512 devices in a mesh: ctx: 128 (over x_hi, z, y), tp: 4 (over x_lo, core).
Axes of the slice: x: 4 (x_hi: 2, x_lo: 2; x = x_hi * 2 + x_lo), y: 4, z: 16, core: 2. Of those that a mesh axis runs over, the one named last changes fastest.
Arguments:
- hidden: bfloat16 [32768, 1024], P('ctx', 'tp'), may hold values from -6 to 6
- bases: int32 [32768], P('ctx'), may hold values from 0 to 3
- base_table: bfloat16 [4, 1024], replicated, may hold values from -6 to 6
- norm_gain: float32 [1024], replicated, may hold values from 0.5 to 1.5
- w_query: bfloat16 [1024, 1024], P(None, 'tp'), may hold values from -0.1875 to 0.1875
- w_key: bfloat16 [1024, 1024], P(None, 'tp'), may hold values from -0.1875 to 0.1875
- w_value: bfloat16 [1024, 1024], P(None, 'tp'), may hold values from -0.1875 to 0.1875
- w_out: bfloat16 [1024, 1024], P('tp'), may hold values from -0.1875 to 0.1875
- filters: float32 [128, 1024], P(None, 'tp'), may hold values from -0.5 to 0.5
Outputs:
- mixed: bfloat16 [32768, 1024], P('ctx', 'tp')
The draws below stay inside these ranges and needn't reach their ends.
All inputs are finite; a program needn't handle non-finite values.
Results may differ from the reference program's by a relative error of at most 0.017.
Values may be sent and summed in bfloat16 or wider, within the bound.
No kernel may reach another device: no remote copies, remote signals or barrier semaphores. Data moves between devices by JAX's collectives and lax.ppermute only.
A program may use at most 64 MiB of HBM per device.

```python
import jax
import jax.numpy as jnp
from jax import lax

D = 1024
K = 128
L = 32768


def set_ends(result, own_key, least, top_value):
    longest = result.shape.index(max(result.shape))
    spots = []
    for shift in (0, 1):
        where = [jax.random.randint(jax.random.fold_in(own_key, axis), (), 0, length) for axis, length in enumerate(result.shape)]
        where[longest] = (where[longest] + shift) % result.shape[longest]
        spots.append(tuple(where))
    return result.at[spots[0]].set(least).at[spots[1]].set(top_value)


def block_levels(key, shape, shards, smallest, largest):
    def one(position, parts):
        draws = jax.random.uniform(jax.random.fold_in(jax.random.fold_in(key, 6), position), (parts,), jnp.float32, smallest / len(shards), largest / len(shards))
        return jnp.repeat(jnp.exp(draws), shape[position] // parts).reshape((-1,) + (1,) * (len(shape) - position - 1))

    gain = one(*shards[0])
    for cut in shards[1:]:
        gain = gain * one(*cut)
    return gain


def gaussian(stream_key, dims, deviation, reach, split=(), kind=jnp.bfloat16):
    array = jax.random.normal(stream_key, dims, jnp.float32) * deviation
    if len(split) > 0:
        array = block_levels(stream_key, dims, split, -0.22, 0.18) * array
    return jnp.clip(array, min=-reach, max=reach).astype(kind)


def setup_inputs(seed: int = 0) -> dict:
    splits = jax.random.split(jax.random.key(seed), 10)
    hidden = gaussian(splits[0], (L, D), 1.0, 6.0, ((0, 128), (1, 4)))
    bases = set_ends(jax.random.randint(splits[1], (L,), 0, 4), jax.random.fold_in(splits[1], 1), 0, 3).astype(jnp.int32)
    base_table = gaussian(splits[2], (4, D), 1.0, 6.0)
    norm_gain = jnp.clip(1.0 + 0.1 * jax.random.normal(splits[3], (D,), jnp.float32), 0.5, 1.5)
    w_query = gaussian(splits[4], (D, D), D ** -0.5, 0.1875, ((1, 4),))
    w_key = gaussian(splits[5], (D, D), D ** -0.5, 0.1875, ((1, 4),))
    w_value = gaussian(splits[6], (D, D), D ** -0.5, 0.1875, ((1, 4),))
    w_out = gaussian(splits[7], (D, D), D ** -0.5, 0.1875, ((0, 4),))
    filters = gaussian(splits[8], (K, D), K ** -0.5, 0.5, ((1, 4),), jnp.float32)
    return dict(hidden=hidden, bases=bases, base_table=base_table, norm_gain=norm_gain, w_query=w_query, w_key=w_key, w_value=w_value, w_out=w_out, filters=filters)


def shift_sum(source, filters, causal):
    length = source.shape[0]
    width = source.shape[1]
    padding = jnp.zeros((K - 1, width), jnp.bfloat16)
    if causal:
        extended = jnp.concatenate([padding, source], axis=0)
    else:
        extended = jnp.concatenate([source, padding], axis=0)

    def add_tap(tap_index, running):
        first_row = K - 1 - tap_index if causal else tap_index
        segment = lax.dynamic_slice_in_dim(extended, first_row, length, 0).astype(jnp.float32)
        tap_row = lax.dynamic_slice_in_dim(filters, tap_index, 1, 0)
        return running + tap_row * segment
    return lax.fori_loop(0, K, add_tap, jnp.zeros((length, width), jnp.float32))

def project(source, weight):
    return jnp.dot(source, weight, preferred_element_type=jnp.float32).astype(jnp.bfloat16)

def reference(hidden, bases, base_table, norm_gain, w_query, w_key, w_value, w_out, filters):
    summed = hidden.astype(jnp.float32) + base_table.astype(jnp.float32)[bases]
    mean_square = lax.optimization_barrier(jnp.mean(summed * summed, axis=1, keepdims=True))
    normed = (summed * lax.rsqrt(mean_square + 1e-06) * norm_gain).astype(jnp.bfloat16)
    flipped = normed[:, ::-1]
    query_fore = project(normed, w_query)
    key_fore = project(normed, w_key)
    value_fore = project(normed, w_value)
    query_back = project(flipped, w_query)
    key_back = project(flipped, w_key)
    value_back = project(flipped, w_value)
    keyval_fore = (key_fore.astype(jnp.float32) * value_fore.astype(jnp.float32)).astype(jnp.bfloat16)
    keyval_back = (key_back.astype(jnp.float32) * value_back.astype(jnp.float32)).astype(jnp.bfloat16)
    mixed_fore = (query_fore.astype(jnp.float32) * shift_sum(keyval_fore, filters, True)).astype(jnp.bfloat16)
    mixed_back = (query_back.astype(jnp.float32) * shift_sum(keyval_back, filters, False)).astype(jnp.bfloat16)
    term = jnp.dot(mixed_fore, w_out, preferred_element_type=jnp.float32)
    term = term + jnp.dot(mixed_back, w_out, preferred_element_type=jnp.float32)[:, ::-1]
    return (hidden.astype(jnp.float32) + term).astype(jnp.bfloat16)
```

```python
import jax
import jax.numpy as jnp
from jax import lax
from jax.experimental import pallas as pl
from jax.experimental.pallas import tpu as pltpu
from jax.sharding import PartitionSpec as P

K = 128
TILE = 8
LANES = 128
GROUP = 4
F32 = jnp.float32
BF16 = jnp.bfloat16
CHIP_PAIRS = [[0, 1], [2, 3]]
CORE_PAIRS = [[0, 2], [1, 3]]


def passed_along(block, axis, distance):
    devices = range(lax.axis_size(axis))
    route = [(i - distance, i) for i in devices if i - distance in devices]
    return lax.ppermute(block, axis, route)


def anti_identity(size):
    rows = lax.broadcasted_iota(jnp.int32, (size, size), 0)
    columns = lax.broadcasted_iota(jnp.int32, (size, size), 1)
    return jnp.where(rows + columns == size - 1, 1.0, 0.0).astype(BF16)


def dot(left, right):
    return jnp.dot(left, right, preferred_element_type=F32)


def columns_reversed(block, out_ref):
    width = 256
    parts = block.shape[1] // width
    flip = anti_identity(width)
    for part in range(parts):
        source = block[:, (parts - 1 - part) * width : (parts - part) * width]
        out_ref[:, part * width : (part + 1) * width] = dot(source, flip).astype(BF16)


def project_kernel(x_ref, bases_ref, table_ref, gain_ref, wk_ref, wv_ref, normed_ref, flipped_ref, kvf_ref, kvb_ref):
    rows = x_ref.shape[0]
    base_rows = lax.broadcasted_iota(jnp.int32, (4, rows), 0)
    one_hot = jnp.where(base_rows == bases_ref[...], 1.0, 0.0).astype(BF16)
    embedded = lax.dot_general(one_hot, table_ref[...], (((0,), (0,)), ((), ())), preferred_element_type=F32)
    summed = x_ref[...].astype(F32) + embedded
    mean_square = jnp.mean(summed * summed, axis=1, keepdims=True)
    normed = (summed * lax.rsqrt(mean_square + 1e-06) * gain_ref[...]).astype(BF16)
    normed_ref[...] = normed
    columns_reversed(normed, flipped_ref)

    def keyval(source):
        key = dot(source, wk_ref[...]).astype(BF16).astype(F32)
        value = dot(source, wv_ref[...]).astype(BF16).astype(F32)
        return (key * value).astype(BF16)

    kvf_ref[...] = keyval(normed)
    kvb_ref[...] = keyval(flipped_ref[...])


def conv_half(source_ref, filters_ref, out_ref, causal):
    half = out_ref.shape[0]
    tiles = half // TILE
    groups = tiles // GROUP
    row = lax.broadcasted_iota(jnp.int32, (TILE, LANES), 0)
    sign = 1 if causal else -1

    def sums(first, count, lanes):
        acc = [[None] * count for _ in range(TILE)]
        for a in range(K // TILE):
            blocks = []
            for i in range(count):
                start = pl.multiple_of((first + i - sign * a) * TILE, TILE)
                blocks.append(source_ref[pl.ds(start, TILE), lanes])
            for b in range(TILE):
                tap = filters_ref[a * TILE + b : a * TILE + b + 1, lanes]
                for i in range(count):
                    product = tap * blocks[i]
                    acc[b][i] = product if a == 0 else acc[b][i] + product
        return acc

    for lane_block in range(out_ref.shape[1] // LANES):
        lanes = slice(lane_block * LANES, (lane_block + 1) * LANES)
        if causal:
            edge = sums(tiles - 1, 1, lanes)
        else:
            edge = sums(tiles, 1, lanes)
        carried = tuple(edge[b][0] for b in range(1, TILE))

        def step(g, carried, lanes=lanes):
            group = g if causal else groups - 1 - g
            first = group * GROUP + (tiles if causal else 0)
            acc = sums(first, GROUP, lanes)
            order = range(GROUP) if causal else range(GROUP - 1, -1, -1)
            before = list(carried)
            for i in order:
                total = acc[0][i]
                for b in range(1, TILE):
                    if causal:
                        picked = jnp.where(row < TILE - b, acc[b][i], before[b - 1])
                        total = total + pltpu.roll(picked, b, 0)
                    else:
                        picked = jnp.where(row >= b, acc[b][i], before[b - 1])
                        total = total + pltpu.roll(picked, TILE - b, 0)
                    before[b - 1] = acc[b][i]
                start = pl.multiple_of((group * GROUP + i) * TILE, TILE)
                out_ref[pl.ds(start, TILE), lanes] = total
            return tuple(before)

        lax.fori_loop(0, groups, step, carried)


def gate(query, conv_out):
    return (query.astype(F32) * conv_out).astype(BF16)


def inner_kernel(normed_ref, flipped_ref, wq_ref, kvf_ref, kvb_ref, filters_ref, wout_ref, qf_ref, qb_ref, mf_ref, mb_ref, wrev_ref, source, conv):
    half = mf_ref.shape[0]
    qf_ref[...] = dot(normed_ref[...], wq_ref[...]).astype(BF16)
    qb_ref[...] = dot(flipped_ref[...], wq_ref[...]).astype(BF16)
    columns_reversed(wout_ref[...], wrev_ref)
    source[...] = kvf_ref[...].astype(F32)
    conv_half(source, filters_ref, conv, True)
    mf_ref[...] = gate(qf_ref[half:], conv[...])
    source[...] = kvb_ref[...].astype(F32)
    conv_half(source, filters_ref, conv, False)
    mb_ref[...] = gate(qb_ref[:half], conv[...])


def outer_kernel(left_ref, right_ref, kvf_ref, kvb_ref, qf_ref, qb_ref, filters_ref, mf_ref, mb_ref, wout_ref, wrev_ref, term_ref, source, conv):
    half = mf_ref.shape[0]
    source[:half] = left_ref[...].astype(F32)
    source[half:] = kvf_ref[:half].astype(F32)
    conv_half(source, filters_ref, conv, True)
    mixed_fore = gate(qf_ref[:half], conv[...])
    source[:half] = kvb_ref[half:].astype(F32)
    source[half:] = right_ref[...].astype(F32)
    conv_half(source, filters_ref, conv, False)
    mixed_back = gate(qb_ref[half:], conv[...])
    term_ref[:half] = (dot(mixed_fore, wout_ref[...]) + dot(mb_ref[...], wrev_ref[...])).astype(BF16)
    term_ref[half:] = (dot(mf_ref[...], wout_ref[...]) + dot(mixed_back, wrev_ref[...])).astype(BF16)


def call(kernel, outs, scratch, flops, bytes_accessed, *operands):
    vmem = pl.BlockSpec(memory_space=pltpu.VMEM)
    return pl.pallas_call(
        kernel,
        out_shape=[jax.ShapeDtypeStruct(shape, kind) for shape, kind in outs],
        in_specs=[vmem] * len(operands),
        out_specs=[vmem] * len(outs),
        scratch_shapes=scratch,
        compiler_params=pltpu.CompilerParams(vmem_limit_bytes=40 * 1024 * 1024),
        cost_estimate=pl.CostEstimate(flops=flops, bytes_accessed=bytes_accessed, transcendentals=0),
    )(*operands)


def on_device(hidden, bases, base_table, norm_gain, w_query, w_key, w_value, w_out, filters):
    rows, channels = hidden.shape
    half = rows // 2
    width = w_query.shape[0]
    gathered = lax.all_gather(hidden, "tp", axis=1, tiled=True)
    normed, flipped, kvf, kvb = call(
        project_kernel,
        [((rows, width), BF16), ((rows, width), BF16), ((rows, channels), BF16), ((rows, channels), BF16)],
        [],
        600_000_000,
        4_000_000,
        gathered,
        bases.reshape(1, rows),
        base_table,
        norm_gain.reshape(1, width),
        w_key,
        w_value,
    )
    left = passed_along(kvf[half:], "ctx", 1)
    right = passed_along(kvb[:half], "ctx", -1)
    scratch = [pltpu.VMEM((rows, channels), F32), pltpu.VMEM((half, channels), F32)]
    qf, qb, mf, mb, w_rev = call(
        inner_kernel,
        [((rows, channels), BF16), ((rows, channels), BF16), ((half, channels), BF16), ((half, channels), BF16), ((channels, width), BF16)],
        scratch,
        2_000_000_000,
        4_000_000,
        normed,
        flipped,
        w_query,
        kvf,
        kvb,
        filters,
        w_out,
    )
    (term,) = call(
        outer_kernel,
        [((rows, width), BF16)],
        scratch,
        2_000_000_000,
        4_000_000,
        left,
        right,
        kvf,
        kvb,
        qf,
        qb,
        filters,
        mf,
        mb,
        w_out,
        w_rev,
    )
    place = lax.axis_index("tp")
    core, chip = place % 2, place // 2
    pair = lax.all_gather(term, "tp", axis_index_groups=CHIP_PAIRS)
    summed = pair[0].astype(F32) + pair[1].astype(F32)
    mine = lax.dynamic_slice_in_dim(summed, place * channels, channels, 1)
    other = lax.dynamic_slice_in_dim(summed, (2 * (1 - chip) + core) * channels, channels, 1)
    both = lax.all_gather(other.astype(BF16), "tp", axis_index_groups=CORE_PAIRS)
    received = jnp.where(chip == 0, both[1], both[0]).astype(F32)
    return (hidden.astype(F32) + mine + received).astype(BF16)


def solution(mesh):
    in_specs = (
        P("ctx", "tp"),
        P("ctx"),
        P(),
        P(),
        P(None, "tp"),
        P(None, "tp"),
        P(None, "tp"),
        P("tp", None),
        P(None, "tp"),
    )
    return jax.shard_map(on_device, mesh=mesh, in_specs=in_specs, out_specs=P("ctx", "tp"), check_vma=False)
```

```python
import jax
import jax.numpy as jnp
from jax import lax
from jax.experimental import pallas as pl
from jax.experimental.pallas import tpu as pltpu
from jax.sharding import PartitionSpec as P

K = 128
TILE = 8
LANES = 128
GROUP = 4
F32 = jnp.float32
BF16 = jnp.bfloat16
CHIP_PAIRS = [[0, 1], [2, 3]]
CORE_PAIRS = [[0, 2], [1, 3]]


def passed_along(block, axis, distance):
    devices = range(lax.axis_size(axis))
    route = [(i - distance, i) for i in devices if i - distance in devices]
    return lax.ppermute(block, axis, route)


def anti_identity(size):
    rows = lax.broadcasted_iota(jnp.int32, (size, size), 0)
    columns = lax.broadcasted_iota(jnp.int32, (size, size), 1)
    return jnp.where(rows + columns == size - 1, 1.0, 0.0).astype(BF16)


def dot(left, right):
    return jnp.dot(left, right, preferred_element_type=F32)


def columns_reversed(block, out_ref):
    width = 256
    parts = block.shape[1] // width
    flip = anti_identity(width)
    for part in range(parts):
        source = block[:, (parts - 1 - part) * width : (parts - part) * width]
        out_ref[:, part * width : (part + 1) * width] = dot(source, flip).astype(BF16)


def project_kernel(x_ref, bases_ref, table_ref, gain_ref, wk_hbm, wv_hbm, normed_ref, flipped_ref, kvf_ref, kvb_ref, wk, wv, arrived):
    key_copy = pltpu.make_async_copy(wk_hbm, wk, arrived.at[0])
    value_copy = pltpu.make_async_copy(wv_hbm, wv, arrived.at[1])
    key_copy.start()
    value_copy.start()
    rows = x_ref.shape[0]
    base_rows = lax.broadcasted_iota(jnp.int32, (4, rows), 0)
    one_hot = jnp.where(base_rows == bases_ref[...], 1.0, 0.0).astype(BF16)
    embedded = lax.dot_general(one_hot, table_ref[...], (((0,), (0,)), ((), ())), preferred_element_type=F32)
    summed = x_ref[...].astype(F32) + embedded
    mean_square = jnp.mean(summed * summed, axis=1, keepdims=True)
    normed = (summed * lax.rsqrt(mean_square + 1e-06) * gain_ref[...]).astype(BF16)
    normed_ref[...] = normed
    columns_reversed(normed, flipped_ref)
    key_copy.wait()
    value_copy.wait()

    def keyval(source):
        key = dot(source, wk[...]).astype(BF16).astype(F32)
        value = dot(source, wv[...]).astype(BF16).astype(F32)
        return (key * value).astype(BF16)

    kvf_ref[...] = keyval(normed)
    kvb_ref[...] = keyval(flipped_ref[...])


def conv_half(source_ref, filters_ref, out_ref, causal):
    half = out_ref.shape[0]
    tiles = half // TILE
    groups = tiles // GROUP
    row = lax.broadcasted_iota(jnp.int32, (TILE, LANES), 0)
    sign = 1 if causal else -1

    def sums(first, count, lanes):
        acc = [[None] * count for _ in range(TILE)]
        for a in range(K // TILE):
            blocks = []
            for i in range(count):
                start = pl.multiple_of((first + i - sign * a) * TILE, TILE)
                blocks.append(source_ref[pl.ds(start, TILE), lanes])
            for b in range(TILE):
                tap = filters_ref[a * TILE + b : a * TILE + b + 1, lanes]
                for i in range(count):
                    product = tap * blocks[i]
                    acc[b][i] = product if a == 0 else acc[b][i] + product
        return acc

    for lane_block in range(out_ref.shape[1] // LANES):
        lanes = slice(lane_block * LANES, (lane_block + 1) * LANES)
        if causal:
            edge = sums(tiles - 1, 1, lanes)
        else:
            edge = sums(tiles, 1, lanes)
        carried = tuple(edge[b][0] for b in range(1, TILE))

        def step(g, carried, lanes=lanes):
            group = g if causal else groups - 1 - g
            first = group * GROUP + (tiles if causal else 0)
            acc = sums(first, GROUP, lanes)
            order = range(GROUP) if causal else range(GROUP - 1, -1, -1)
            before = list(carried)
            for i in order:
                total = acc[0][i]
                for b in range(1, TILE):
                    if causal:
                        picked = jnp.where(row < TILE - b, acc[b][i], before[b - 1])
                        total = total + pltpu.roll(picked, b, 0)
                    else:
                        picked = jnp.where(row >= b, acc[b][i], before[b - 1])
                        total = total + pltpu.roll(picked, TILE - b, 0)
                    before[b - 1] = acc[b][i]
                start = pl.multiple_of((group * GROUP + i) * TILE, TILE)
                out_ref[pl.ds(start, TILE), lanes] = total
            return tuple(before)

        lax.fori_loop(0, groups, step, carried)


def gate(query, conv_out):
    return (query.astype(F32) * conv_out).astype(BF16)


def inner_kernel(normed_ref, flipped_ref, wq_ref, kvf_ref, kvb_ref, filters_ref, wout_ref, qf_ref, qb_ref, mf_ref, mb_ref, wrev_ref, source, conv):
    half = mf_ref.shape[0]
    qf_ref[...] = dot(normed_ref[...], wq_ref[...]).astype(BF16)
    qb_ref[...] = dot(flipped_ref[...], wq_ref[...]).astype(BF16)
    columns_reversed(wout_ref[...], wrev_ref)
    source[...] = kvf_ref[...].astype(F32)
    conv_half(source, filters_ref, conv, True)
    mf_ref[...] = gate(qf_ref[half:], conv[...])
    source[...] = kvb_ref[...].astype(F32)
    conv_half(source, filters_ref, conv, False)
    mb_ref[...] = gate(qb_ref[:half], conv[...])


def outer_kernel(left_ref, right_ref, kvf_ref, kvb_ref, qf_ref, qb_ref, filters_ref, mf_ref, mb_ref, wout_ref, wrev_ref, keep_ref, send_ref, source, conv, fore, back):
    half = mf_ref.shape[0]
    width = keep_ref.shape[1] // 2
    source[:half] = left_ref[...].astype(F32)
    source[half:] = kvf_ref[:half].astype(F32)
    conv_half(source, filters_ref, conv, True)
    fore[:half] = gate(qf_ref[:half], conv[...])
    fore[half:] = mf_ref[...]
    source[:half] = kvb_ref[half:].astype(F32)
    source[half:] = right_ref[...].astype(F32)
    conv_half(source, filters_ref, conv, False)
    back[:half] = mb_ref[...]
    back[half:] = gate(qb_ref[half:], conv[...])
    place = lax.axis_index("tp")
    core = lax.rem(place, 2)
    chip = place // 2
    for out_ref, at_core in ((send_ref, 1 - core), (keep_ref, core)):
        for part, at_chip in enumerate((chip, 1 - chip)):
            columns = pl.ds(pl.multiple_of((2 * at_chip + at_core) * width, width), width)
            total = dot(fore[...], wout_ref[:, columns]) + dot(back[...], wrev_ref[:, columns])
            out_ref[:, part * width : (part + 1) * width] = total.astype(out_ref.dtype)


def call(kernel, outs, scratch, flops, bytes_accessed, operands, in_hbm=()):
    vmem = pl.BlockSpec(memory_space=pltpu.VMEM)
    anywhere = pl.BlockSpec(memory_space=pl.ANY)
    return pl.pallas_call(
        kernel,
        out_shape=[jax.ShapeDtypeStruct(shape, kind) for shape, kind in outs],
        in_specs=[anywhere if i in in_hbm else vmem for i in range(len(operands))],
        out_specs=[vmem] * len(outs),
        scratch_shapes=scratch,
        compiler_params=pltpu.CompilerParams(vmem_limit_bytes=40 * 1024 * 1024),
        cost_estimate=pl.CostEstimate(flops=flops, bytes_accessed=bytes_accessed, transcendentals=0),
    )(*operands)


def on_device(hidden, bases, base_table, norm_gain, w_query, w_key, w_value, w_out, filters):
    rows, channels = hidden.shape
    half = rows // 2
    width = w_query.shape[0]
    gathered = lax.all_gather(hidden, "tp", axis=1, tiled=True)
    normed, flipped, kvf, kvb = call(
        project_kernel,
        [((rows, width), BF16), ((rows, width), BF16), ((rows, channels), BF16), ((rows, channels), BF16)],
        [pltpu.VMEM(w_key.shape, BF16), pltpu.VMEM(w_value.shape, BF16), pltpu.SemaphoreType.DMA((2,))],
        600_000_000,
        4_000_000,
        (gathered, bases.reshape(1, rows), base_table, norm_gain.reshape(1, width), w_key, w_value),
        in_hbm=(4, 5),
    )
    left = passed_along(kvf[half:], "ctx", 1)
    right = passed_along(kvb[:half], "ctx", -1)
    scratch = [pltpu.VMEM((rows, channels), F32), pltpu.VMEM((half, channels), F32)]
    qf, qb, mf, mb, w_rev = call(
        inner_kernel,
        [((rows, channels), BF16), ((rows, channels), BF16), ((half, channels), BF16), ((half, channels), BF16), ((channels, width), BF16)],
        scratch,
        2_000_000_000,
        4_000_000,
        (normed, flipped, w_query, kvf, kvb, filters, w_out),
    )
    keep, send = call(
        outer_kernel,
        [((rows, 2 * channels), F32), ((rows, 2 * channels), BF16)],
        scratch + [pltpu.VMEM((rows, channels), BF16), pltpu.VMEM((rows, channels), BF16)],
        2_000_000_000,
        4_000_000,
        (left, right, kvf, kvb, qf, qb, filters, mf, mb, w_out, w_rev),
    )
    place = lax.axis_index("tp")
    pair = lax.all_gather(send, "tp", axis_index_groups=CHIP_PAIRS)
    summed = keep + jnp.where(place % 2 == 0, pair[1], pair[0]).astype(F32)
    both = lax.all_gather(summed[:, channels:].astype(BF16), "tp", axis_index_groups=CORE_PAIRS)
    received = jnp.where(place < 2, both[1], both[0]).astype(F32)
    return (hidden.astype(F32) + summed[:, :channels] + received).astype(BF16)


def solution(mesh):
    in_specs = (
        P("ctx", "tp"),
        P("ctx"),
        P(),
        P(),
        P(None, "tp"),
        P(None, "tp"),
        P(None, "tp"),
        P("tp", None),
        P(None, "tp"),
    )
    return jax.shard_map(on_device, mesh=mesh, in_specs=in_specs, out_specs=P("ctx", "tp"), check_vma=False)
```

```python
import jax
import jax.numpy as jnp
from jax import lax
from jax.experimental import pallas as pl
from jax.experimental.pallas import tpu as pltpu
from jax.sharding import PartitionSpec as P

K = 128
TILE = 8
LANES = 128
GROUP = 4
F32 = jnp.float32
BF16 = jnp.bfloat16
CHIP_PAIRS = [[0, 1], [2, 3]]
CORE_PAIRS = [[0, 2], [1, 3]]


def passed_along(block, axis, distance):
    devices = range(lax.axis_size(axis))
    route = [(i - distance, i) for i in devices if i - distance in devices]
    return lax.ppermute(block, axis, route)


def anti_identity(size):
    rows = lax.broadcasted_iota(jnp.int32, (size, size), 0)
    columns = lax.broadcasted_iota(jnp.int32, (size, size), 1)
    return jnp.where(rows + columns == size - 1, 1.0, 0.0).astype(BF16)


def dot(left, right):
    return jnp.dot(left, right, preferred_element_type=F32)


def columns_reversed(block, out_ref):
    width = 256
    parts = block.shape[1] // width
    flip = anti_identity(width)
    for part in range(parts):
        source = block[:, (parts - 1 - part) * width : (parts - part) * width]
        out_ref[:, part * width : (part + 1) * width] = dot(source, flip).astype(BF16)


def project_kernel(x_ref, bases_ref, table_ref, gain_ref, wk_ref, wv_hbm, normed_ref, flipped_ref, kvf_ref, kvb_ref, wv, arrived):
    value_copy = pltpu.make_async_copy(wv_hbm, wv, arrived)
    value_copy.start()
    rows = x_ref.shape[0]
    base_rows = lax.broadcasted_iota(jnp.int32, (4, rows), 0)
    one_hot = jnp.where(base_rows == bases_ref[...], 1.0, 0.0).astype(BF16)
    embedded = lax.dot_general(one_hot, table_ref[...], (((0,), (0,)), ((), ())), preferred_element_type=F32)
    summed = x_ref[...].astype(F32) + embedded
    mean_square = jnp.mean(summed * summed, axis=1, keepdims=True)
    normed = (summed * lax.rsqrt(mean_square + 1e-06) * gain_ref[...]).astype(BF16)
    normed_ref[...] = normed
    columns_reversed(normed, flipped_ref)
    key_fore = dot(normed, wk_ref[...]).astype(BF16).astype(F32)
    key_back = dot(flipped_ref[...], wk_ref[...]).astype(BF16).astype(F32)
    value_copy.wait()
    value_fore = dot(normed, wv[...]).astype(BF16).astype(F32)
    value_back = dot(flipped_ref[...], wv[...]).astype(BF16).astype(F32)
    kvf_ref[...] = (key_fore * value_fore).astype(BF16)
    kvb_ref[...] = (key_back * value_back).astype(BF16)


def conv_half(source_ref, filters_ref, out_ref, causal):
    half = out_ref.shape[0]
    tiles = half // TILE
    groups = tiles // GROUP
    row = lax.broadcasted_iota(jnp.int32, (TILE, LANES), 0)
    sign = 1 if causal else -1

    def sums(first, count, lanes):
        acc = [[None] * count for _ in range(TILE)]
        for a in range(K // TILE):
            blocks = []
            for i in range(count):
                start = pl.multiple_of((first + i - sign * a) * TILE, TILE)
                blocks.append(source_ref[pl.ds(start, TILE), lanes])
            for b in range(TILE):
                tap = filters_ref[a * TILE + b : a * TILE + b + 1, lanes]
                for i in range(count):
                    product = tap * blocks[i]
                    acc[b][i] = product if a == 0 else acc[b][i] + product
        return acc

    for lane_block in range(out_ref.shape[1] // LANES):
        lanes = slice(lane_block * LANES, (lane_block + 1) * LANES)
        if causal:
            edge = sums(tiles - 1, 1, lanes)
        else:
            edge = sums(tiles, 1, lanes)
        carried = tuple(edge[b][0] for b in range(1, TILE))

        def step(g, carried, lanes=lanes):
            group = g if causal else groups - 1 - g
            first = group * GROUP + (tiles if causal else 0)
            acc = sums(first, GROUP, lanes)
            order = range(GROUP) if causal else range(GROUP - 1, -1, -1)
            before = list(carried)
            for i in order:
                total = acc[0][i]
                for b in range(1, TILE):
                    if causal:
                        picked = jnp.where(row < TILE - b, acc[b][i], before[b - 1])
                        total = total + pltpu.roll(picked, b, 0)
                    else:
                        picked = jnp.where(row >= b, acc[b][i], before[b - 1])
                        total = total + pltpu.roll(picked, TILE - b, 0)
                    before[b - 1] = acc[b][i]
                start = pl.multiple_of((group * GROUP + i) * TILE, TILE)
                out_ref[pl.ds(start, TILE), lanes] = total
            return tuple(before)

        lax.fori_loop(0, groups, step, carried)


def gate(query, conv_out):
    return (query.astype(F32) * conv_out).astype(BF16)


def reached_late():
    return lax.axis_index("ctx") == lax.axis_size("ctx") // 2


def inner(normed_ref, flipped_ref, wq_ref, kvf_ref, kvb_ref, filters_ref, wout_ref, outs, source, conv):
    qf_ref, qb_ref, mf_ref, mb_ref, wrev_ref = outs
    half = mf_ref.shape[0]
    qf_ref[...] = dot(normed_ref[...], wq_ref[...]).astype(BF16)
    qb_ref[...] = dot(flipped_ref[...], wq_ref[...]).astype(BF16)
    columns_reversed(wout_ref[...], wrev_ref)
    source[...] = kvf_ref[...].astype(F32)
    conv_half(source, filters_ref, conv, True)
    mf_ref[...] = gate(qf_ref[half:], conv[...])
    source[...] = kvb_ref[...].astype(F32)
    conv_half(source, filters_ref, conv, False)
    mb_ref[...] = gate(qb_ref[:half], conv[...])


def early_kernel(normed_ref, flipped_ref, wq_ref, kvf_ref, kvb_ref, filters_ref, wout_ref, last_ref, first_ref, *rest):
    half = last_ref.shape[0]
    last_ref[...] = kvf_ref[half:]
    first_ref[...] = kvb_ref[:half]

    @pl.when(reached_late())
    def _():
        inner(normed_ref, flipped_ref, wq_ref, kvf_ref, kvb_ref, filters_ref, wout_ref, rest[:5], *rest[5:])


def inner_kernel(normed_ref, flipped_ref, wq_ref, kvf_ref, kvb_ref, filters_ref, wout_ref, *rest):
    early, outs, scratch = rest[:5], rest[5:10], rest[10:]

    @pl.when(reached_late())
    def _():
        for done_ref, out_ref in zip(early, outs):
            out_ref[...] = done_ref[...]

    @pl.when(jnp.logical_not(reached_late()))
    def _():
        inner(normed_ref, flipped_ref, wq_ref, kvf_ref, kvb_ref, filters_ref, wout_ref, outs, *scratch)


def outer_kernel(left_ref, right_ref, kvf_ref, kvb_ref, qf_ref, qb_ref, filters_ref, mf_ref, mb_ref, wout_ref, wrev_ref, keep_ref, send_ref, source, conv, fore, back):
    half = mf_ref.shape[0]
    width = keep_ref.shape[1] // 2
    source[:half] = left_ref[...].astype(F32)
    source[half:] = kvf_ref[:half].astype(F32)
    conv_half(source, filters_ref, conv, True)
    fore[:half] = gate(qf_ref[:half], conv[...])
    fore[half:] = mf_ref[...]
    source[:half] = kvb_ref[half:].astype(F32)
    source[half:] = right_ref[...].astype(F32)
    conv_half(source, filters_ref, conv, False)
    back[:half] = mb_ref[...]
    back[half:] = gate(qb_ref[half:], conv[...])
    place = lax.axis_index("tp")
    core = lax.rem(place, 2)
    chip = place // 2
    for out_ref, at_core in ((send_ref, 1 - core), (keep_ref, core)):
        for part, at_chip in enumerate((chip, 1 - chip)):
            columns = pl.ds(pl.multiple_of((2 * at_chip + at_core) * width, width), width)
            total = dot(fore[...], wout_ref[:, columns]) + dot(back[...], wrev_ref[:, columns])
            out_ref[:, part * width : (part + 1) * width] = total.astype(out_ref.dtype)


def call(kernel, outs, scratch, flops, bytes_accessed, operands, in_hbm=()):
    vmem = pl.BlockSpec(memory_space=pltpu.VMEM)
    hbm = pl.BlockSpec(memory_space=pltpu.HBM)
    operands = [pltpu.with_memory_space_constraint(x, pltpu.HBM) if i in in_hbm else x for i, x in enumerate(operands)]
    return pl.pallas_call(
        kernel,
        out_shape=[jax.ShapeDtypeStruct(shape, kind) for shape, kind in outs],
        in_specs=[hbm if i in in_hbm else vmem for i in range(len(operands))],
        out_specs=[vmem] * len(outs),
        scratch_shapes=scratch,
        compiler_params=pltpu.CompilerParams(vmem_limit_bytes=40 * 1024 * 1024),
        cost_estimate=pl.CostEstimate(flops=flops, bytes_accessed=bytes_accessed, transcendentals=0),
    )(*operands)


def on_device(hidden, bases, base_table, norm_gain, w_query, w_key, w_value, w_out, filters):
    rows, channels = hidden.shape
    half = rows // 2
    width = w_query.shape[0]
    gathered = lax.all_gather(hidden, "tp", axis=1, tiled=True)
    normed, flipped, kvf, kvb = call(
        project_kernel,
        [((rows, width), BF16), ((rows, width), BF16), ((rows, channels), BF16), ((rows, channels), BF16)],
        [pltpu.VMEM(w_value.shape, BF16), pltpu.SemaphoreType.DMA(())],
        600_000_000,
        4_000_000,
        (gathered, bases.reshape(1, rows), base_table, norm_gain.reshape(1, width), w_key, w_value),
        in_hbm=(5,),
    )
    scratch = [pltpu.VMEM((rows, channels), F32), pltpu.VMEM((half, channels), F32)]
    inner_outs = [((rows, channels), BF16), ((rows, channels), BF16), ((half, channels), BF16), ((half, channels), BF16), ((channels, width), BF16)]
    inner_operands = (normed, flipped, w_query, kvf, kvb, filters, w_out)
    last, first, *early = call(early_kernel, [((half, channels), BF16)] * 2 + inner_outs, scratch, 1_000_000, 300_000, inner_operands)
    left = passed_along(last, "ctx", 1)
    right = passed_along(first, "ctx", -1)
    qf, qb, mf, mb, w_rev = call(inner_kernel, inner_outs, scratch, 2_000_000_000, 4_000_000, inner_operands + tuple(early))
    keep, send = call(
        outer_kernel,
        [((rows, 2 * channels), F32), ((rows, 2 * channels), BF16)],
        scratch + [pltpu.VMEM((rows, channels), BF16), pltpu.VMEM((rows, channels), BF16)],
        2_000_000_000,
        4_000_000,
        (left, right, kvf, kvb, qf, qb, filters, mf, mb, w_out, w_rev),
    )
    place = lax.axis_index("tp")
    pair = lax.all_gather(send, "tp", axis_index_groups=CHIP_PAIRS)
    summed = keep + jnp.where(place % 2 == 0, pair[1], pair[0]).astype(F32)
    both = lax.all_gather(summed[:, channels:].astype(BF16), "tp", axis_index_groups=CORE_PAIRS)
    received = jnp.where(place < 2, both[1], both[0]).astype(F32)
    return (hidden.astype(F32) + summed[:, :channels] + received).astype(BF16)


def solution(mesh):
    in_specs = (
        P("ctx", "tp"),
        P("ctx"),
        P(),
        P(),
        P(None, "tp"),
        P(None, "tp"),
        P(None, "tp"),
        P("tp", None),
        P(None, "tp"),
    )
    return jax.shard_map(on_device, mesh=mesh, in_specs=in_specs, out_specs=P("ctx", "tp"), check_vma=False)
```

```python
import jax
import jax.numpy as jnp
from jax import lax
from jax.experimental import pallas as pl
from jax.experimental.pallas import tpu as pltpu
from jax.sharding import PartitionSpec as P

K = 128
TILE = 8
STEPS = K // TILE
LANES = 128
GROUP = 4
F32 = jnp.float32
BF16 = jnp.bfloat16
CHIP_PAIRS = [[0, 1], [2, 3]]
CORE_PAIRS = [[0, 2], [1, 3]]


def passed_along(block, axis, distance):
    devices = range(lax.axis_size(axis))
    route = [(i - distance, i) for i in devices if i - distance in devices]
    return lax.ppermute(block, axis, route)


def anti_identity(size):
    rows = lax.broadcasted_iota(jnp.int32, (size, size), 0)
    columns = lax.broadcasted_iota(jnp.int32, (size, size), 1)
    return jnp.where(rows + columns == size - 1, 1.0, 0.0).astype(BF16)


def dot(left, right):
    return jnp.dot(left, right, preferred_element_type=F32)


def columns_reversed(block, out_ref):
    width = 256
    parts = block.shape[1] // width
    flip = anti_identity(width)
    for part in range(parts):
        source = block[:, (parts - 1 - part) * width : (parts - part) * width]
        out_ref[:, part * width : (part + 1) * width] = dot(source, flip).astype(BF16)


def project_kernel(x_ref, bases_ref, table_ref, gain_ref, wk_ref, wv_hbm, normed_ref, flipped_ref, kvf_ref, kvb_ref, wv, arrived):
    value_copy = pltpu.make_async_copy(wv_hbm, wv, arrived)
    value_copy.start()
    rows = x_ref.shape[0]
    base_rows = lax.broadcasted_iota(jnp.int32, (4, rows), 0)
    one_hot = jnp.where(base_rows == bases_ref[...], 1.0, 0.0).astype(BF16)
    embedded = lax.dot_general(one_hot, table_ref[...], (((0,), (0,)), ((), ())), preferred_element_type=F32)
    summed = x_ref[...].astype(F32) + embedded
    mean_square = jnp.mean(summed * summed, axis=1, keepdims=True)
    normed = (summed * lax.rsqrt(mean_square + 1e-06) * gain_ref[...]).astype(BF16)
    normed_ref[...] = normed
    columns_reversed(normed, flipped_ref)
    key_fore = dot(normed, wk_ref[...]).astype(BF16).astype(F32)
    key_back = dot(flipped_ref[...], wk_ref[...]).astype(BF16).astype(F32)
    value_copy.wait()
    value_fore = dot(normed, wv[...]).astype(BF16).astype(F32)
    value_back = dot(flipped_ref[...], wv[...]).astype(BF16).astype(F32)
    kvf_ref[...] = (key_fore * value_fore).astype(BF16)
    kvb_ref[...] = (key_back * value_back).astype(BF16)


def tap_sums(source_ref, filters_ref, lanes, plan):
    acc = [[None] * len(plan) for _ in range(TILE)]
    for a in range(STEPS):
        starts = {i: dict(pairs)[a] for i, pairs in enumerate(plan) if a in dict(pairs)}
        blocks = {i: source_ref[pl.ds(start, TILE), lanes] for i, start in starts.items()}
        for b in range(TILE) if starts else ():
            tap = filters_ref[a * TILE + b : a * TILE + b + 1, lanes]
            for i, block in blocks.items():
                product = tap * block
                acc[b][i] = product if acc[b][i] is None else acc[b][i] + product
    return acc


def moved_sum(here, before, causal):
    row = lax.broadcasted_iota(jnp.int32, (TILE, LANES), 0)
    total = here[0]
    for b in range(1, TILE):
        if causal:
            picked = jnp.where(row < TILE - b, here[b], before[b])
            piece = pltpu.roll(picked, b, 0)
        else:
            picked = jnp.where(row >= b, here[b], before[b])
            piece = pltpu.roll(picked, TILE - b, 0)
        total = total + piece
    return total


def conv_local(source_ref, filters_ref, out_ref, causal):
    tiles = source_ref.shape[0] // TILE
    zero = jnp.zeros((TILE, LANES), F32)

    def row_of(u):
        return (u if causal else tiles - 1 - u) * TILE

    for lane_block in range(source_ref.shape[1] // LANES):
        lanes = slice(lane_block * LANES, (lane_block + 1) * LANES)

        def group(first, before, lanes, at):
            plan = [[(a, at(first + i - a)) for a in range(STEPS) if not isinstance(first, int) or first + i >= a] for i in range(GROUP)]
            acc = tap_sums(source_ref, filters_ref, lanes, plan)
            for i in range(GROUP):
                here = [acc[b][i] for b in range(TILE)]
                out_ref[pl.ds(at(first + i), TILE), lanes] = moved_sum(here, before, causal)
                before = here
            return before

        before = [zero] * TILE
        for g in range(STEPS // GROUP):
            before = group(g * GROUP, before, lanes, row_of)

        def step(g, carried, lanes=lanes, group=group):
            before = group(g * GROUP, [zero, *carried], lanes, lambda u: pl.multiple_of(row_of(u), TILE))
            return tuple(before[1:])

        lax.fori_loop(STEPS // GROUP, tiles // GROUP, step, tuple(before[1:]))


def conv_halo(source_ref, filters_ref, out_ref, causal):
    tiles = source_ref.shape[0] // TILE
    zero = jnp.zeros((TILE, LANES), F32)

    def row_of(u):
        return (u if causal else tiles - 1 - u) * TILE

    for lane_block in range(source_ref.shape[1] // LANES):
        lanes = slice(lane_block * LANES, (lane_block + 1) * LANES)
        before = [zero] * TILE
        for first in range(-1, tiles - 1, GROUP):
            plan = [[(a, row_of(tiles + u - a)) for a in range(u + 1, STEPS)] for u in range(first, first + GROUP)]
            acc = tap_sums(source_ref, filters_ref, lanes, plan)
            for i, u in enumerate(range(first, first + GROUP)):
                here = [acc[b][i] for b in range(TILE)]
                if u >= 0:
                    rows = slice(row_of(u), row_of(u) + TILE)
                    out_ref[rows, lanes] = out_ref[rows, lanes] + moved_sum(here, before, causal)
                before = here
        rows = slice(row_of(tiles - 1), row_of(tiles - 1) + TILE)
        out_ref[rows, lanes] = out_ref[rows, lanes] + moved_sum([zero] * TILE, before, causal)


def gate(query, conv_out):
    return (query.astype(F32) * conv_out).astype(BF16)


def reached_late():
    return lax.axis_index("ctx") == lax.axis_size("ctx") // 2


def inner(normed_ref, flipped_ref, wq_ref, kvf_ref, kvb_ref, filters_ref, wout_ref, outs, query, source, conv):
    qf_ref, qb_ref, pf_ref, pb_ref, tf_ref, tb_ref, wf_ref, wb_ref = outs
    half = qf_ref.shape[0]
    width = kvf_ref.shape[1]
    place = lax.axis_index("tp")
    core = lax.rem(place, 2)
    chip = place // 2
    flip = anti_identity(width)
    for part, (at_core, at_chip) in enumerate(((core, chip), (core, 1 - chip), (1 - core, chip), (1 - core, 1 - chip))):
        number = 2 * at_chip + at_core
        columns = slice(part * width, (part + 1) * width)
        wf_ref[:, columns] = wout_ref[:, pl.ds(pl.multiple_of(number * width, width), width)]
        wb_ref[:, columns] = dot(wout_ref[:, pl.ds(pl.multiple_of((3 - number) * width, width), width)], flip).astype(BF16)

    query[...] = dot(normed_ref[...], wq_ref[...]).astype(BF16)
    qf_ref[...] = query[:half]
    source[...] = kvf_ref[...].astype(F32)
    conv_local(source, filters_ref, conv, True)
    pf_ref[...] = conv[:half]
    tf_ref[...] = dot(gate(query[half:], conv[half:]), wf_ref[...])

    query[...] = dot(flipped_ref[...], wq_ref[...]).astype(BF16)
    qb_ref[...] = query[half:]
    source[...] = kvb_ref[...].astype(F32)
    conv_local(source, filters_ref, conv, False)
    pb_ref[...] = conv[half:]
    tb_ref[...] = dot(gate(query[:half], conv[:half]), wb_ref[...])


def early_kernel(normed_ref, flipped_ref, wq_ref, kvf_ref, kvb_ref, filters_ref, wout_ref, last_ref, first_ref, *rest):
    half = last_ref.shape[0]
    last_ref[...] = kvf_ref[half:]
    first_ref[...] = kvb_ref[:half]

    @pl.when(reached_late())
    def _():
        inner(normed_ref, flipped_ref, wq_ref, kvf_ref, kvb_ref, filters_ref, wout_ref, rest[:8], *rest[8:])


def inner_kernel(normed_ref, flipped_ref, wq_ref, kvf_ref, kvb_ref, filters_ref, wout_ref, *rest):
    early, outs, scratch = rest[:8], rest[8:16], rest[16:]

    @pl.when(reached_late())
    def _():
        for done_ref, out_ref in zip(early, outs):
            out_ref[...] = done_ref[...]

    @pl.when(jnp.logical_not(reached_late()))
    def _():
        inner(normed_ref, flipped_ref, wq_ref, kvf_ref, kvb_ref, filters_ref, wout_ref, outs, *scratch)


def outer(halo_ref, q_ref, part_ref, term_ref, w_ref, filters_ref, source, conv, causal):
    source[...] = halo_ref[...].astype(F32)
    conv[...] = part_ref[...]
    conv_halo(source, filters_ref, conv, causal)
    return term_ref[...] + dot(gate(q_ref[...], conv[...]), w_ref[...])


def fore_kernel(left_ref, qf_ref, pf_ref, tb_ref, wf_ref, filters_ref, keep_ref, send_ref, source, conv):
    width = keep_ref.shape[1]
    total = outer(left_ref, qf_ref, pf_ref, tb_ref, wf_ref, filters_ref, source, conv, True)
    keep_ref[...] = total[:, :width]
    send_ref[...] = total[:, width:].astype(BF16)


def back_kernel(right_ref, qb_ref, pb_ref, tf_ref, wb_ref, filters_ref, low_keep_ref, low_send_ref, keep_ref, send_ref, source, conv):
    half, width = low_keep_ref.shape
    total = outer(right_ref, qb_ref, pb_ref, tf_ref, wb_ref, filters_ref, source, conv, False)
    keep_ref[:half] = low_keep_ref[...]
    send_ref[:half] = low_send_ref[...]
    keep_ref[half:] = total[:, :width]
    send_ref[half:] = total[:, width:].astype(BF16)


def call(kernel, outs, scratch, flops, bytes_accessed, operands, in_hbm=()):
    vmem = pl.BlockSpec(memory_space=pltpu.VMEM)
    hbm = pl.BlockSpec(memory_space=pltpu.HBM)
    operands = [pltpu.with_memory_space_constraint(x, pltpu.HBM) if i in in_hbm else x for i, x in enumerate(operands)]
    return pl.pallas_call(
        kernel,
        out_shape=[jax.ShapeDtypeStruct(shape, kind) for shape, kind in outs],
        in_specs=[hbm if i in in_hbm else vmem for i in range(len(operands))],
        out_specs=[vmem] * len(outs),
        scratch_shapes=scratch,
        compiler_params=pltpu.CompilerParams(vmem_limit_bytes=40 * 1024 * 1024),
        cost_estimate=pl.CostEstimate(flops=flops, bytes_accessed=bytes_accessed, transcendentals=0),
    )(*operands)


def on_device(hidden, bases, base_table, norm_gain, w_query, w_key, w_value, w_out, filters):
    rows, channels = hidden.shape
    half = rows // 2
    width = w_query.shape[0]
    gathered = lax.all_gather(hidden, "tp", axis=1, tiled=True)
    normed, flipped, kvf, kvb = call(
        project_kernel,
        [((rows, width), BF16), ((rows, width), BF16), ((rows, channels), BF16), ((rows, channels), BF16)],
        [pltpu.VMEM(w_value.shape, BF16), pltpu.SemaphoreType.DMA(())],
        600_000_000,
        4_000_000,
        (gathered, bases.reshape(1, rows), base_table, norm_gain.reshape(1, width), w_key, w_value),
        in_hbm=(5,),
    )
    edge = ((half, channels), BF16)
    partial = ((half, channels), F32)
    term = ((half, width), F32)
    weight = ((channels, width), BF16)
    inner_outs = [edge, edge, partial, partial, term, term, weight, weight]
    scratch = [pltpu.VMEM((rows, channels), BF16), pltpu.VMEM((rows, channels), F32), pltpu.VMEM((rows, channels), F32)]
    operands = (normed, flipped, w_query, kvf, kvb, filters, w_out)
    last, first, *early = call(early_kernel, [edge, edge] + inner_outs, scratch, 1_000_000, 300_000, operands)
    left = passed_along(last, "ctx", 1)
    right = passed_along(first, "ctx", -1)
    qf, qb, pf, pb, tf, tb, wf, wb = call(inner_kernel, inner_outs, scratch, 2_000_000_000, 4_000_000, operands + tuple(early))
    scratch = [pltpu.VMEM((half, channels), F32), pltpu.VMEM((half, channels), F32)]
    low = call(
        fore_kernel,
        [((half, 2 * channels), F32), ((half, 2 * channels), BF16)],
        scratch,
        500_000_000,
        2_000_000,
        (left, qf, pf, tb, wf, filters),
    )
    keep, send = call(
        back_kernel,
        [((rows, 2 * channels), F32), ((rows, 2 * channels), BF16)],
        scratch,
        500_000_000,
        2_000_000,
        (right, qb, pb, tf, wb, filters, *low),
    )
    place = lax.axis_index("tp")
    pair = lax.all_gather(send, "tp", axis_index_groups=CHIP_PAIRS)
    summed = keep + jnp.where(place % 2 == 0, pair[1], pair[0]).astype(F32)
    both = lax.all_gather(summed[:, channels:].astype(BF16), "tp", axis_index_groups=CORE_PAIRS)
    received = jnp.where(place < 2, both[1], both[0]).astype(F32)
    return (hidden.astype(F32) + summed[:, :channels] + received).astype(BF16)


def solution(mesh):
    in_specs = (
        P("ctx", "tp"),
        P("ctx"),
        P(),
        P(),
        P(None, "tp"),
        P(None, "tp"),
        P(None, "tp"),
        P("tp", None),
        P(None, "tp"),
    )
    return jax.shard_map(on_device, mesh=mesh, in_specs=in_specs, out_specs=P("ctx", "tp"), check_vma=False)
```

```python
import jax
import jax.numpy as jnp
from jax import lax
from jax.experimental import pallas as pl
from jax.experimental.pallas import tpu as pltpu
from jax.sharding import PartitionSpec as P

K = 128
TILE = 8
STEPS = K // TILE
LANES = 128
GROUP = 4
F32 = jnp.float32
BF16 = jnp.bfloat16
CHIP_PAIRS = [[0, 1], [2, 3]]
CORE_PAIRS = [[0, 2], [1, 3]]


def passed_along(block, axis, distance):
    devices = range(lax.axis_size(axis))
    route = [(i - distance, i) for i in devices if i - distance in devices]
    return lax.ppermute(block, axis, route)


def anti_identity(size):
    rows = lax.broadcasted_iota(jnp.int32, (size, size), 0)
    columns = lax.broadcasted_iota(jnp.int32, (size, size), 1)
    return jnp.where(rows + columns == size - 1, 1.0, 0.0).astype(BF16)


def dot(left, right):
    return jnp.dot(left, right, preferred_element_type=F32)


def columns_reversed(block, flip, out_ref):
    width = flip.shape[0]
    parts = block.shape[1] // width
    for part in range(parts):
        source = block[:, (parts - 1 - part) * width : (parts - part) * width]
        out_ref[:, part * width : (part + 1) * width] = dot(source, flip).astype(BF16)


def keyval(source, wk_ref, wv_ref):
    key = dot(source, wk_ref[...]).astype(BF16).astype(F32)
    value = dot(source, wv_ref[...]).astype(BF16).astype(F32)
    return (key * value).astype(BF16)


def prepare_kernel(bases_hbm, one_hot_ref, flip_ref, bases_ref, arrived):
    copy = pltpu.make_async_copy(bases_hbm, bases_ref, arrived)
    copy.start()
    flip_ref[...] = anti_identity(flip_ref.shape[0])
    copy.wait()
    base_rows = lax.broadcasted_iota(jnp.int32, one_hot_ref.shape, 0)
    one_hot_ref[...] = jnp.where(base_rows == bases_ref[...], 1.0, 0.0).astype(BF16)


def project_kernel(x_ref, one_hot_ref, table_ref, gain_ref, wk_ref, wv_ref, flip_ref, normed_ref, flipped_ref, kvf_ref, kvb_ref):
    half = kvf_ref.shape[0]
    embedded = lax.dot_general(one_hot_ref[...], table_ref[...], (((0,), (0,)), ((), ())), preferred_element_type=F32)
    summed = x_ref[...].astype(F32) + embedded
    mean_square = jnp.mean(summed * summed, axis=1, keepdims=True)
    normed = (summed * lax.rsqrt(mean_square + 1e-06) * gain_ref[...]).astype(BF16)
    normed_ref[...] = normed
    columns_reversed(normed[:half], flip_ref[...], flipped_ref)
    kvf_ref[...] = keyval(normed[half:], wk_ref, wv_ref)
    kvb_ref[...] = keyval(flipped_ref[...], wk_ref, wv_ref)


def tap_sums(source_ref, filters_ref, lanes, plan):
    acc = [[None] * len(plan) for _ in range(TILE)]
    for a in range(STEPS):
        starts = {i: dict(pairs)[a] for i, pairs in enumerate(plan) if a in dict(pairs)}
        blocks = {i: source_ref[pl.ds(start, TILE), lanes] for i, start in starts.items()}
        for b in range(TILE) if starts else ():
            tap = filters_ref[a * TILE + b : a * TILE + b + 1, lanes]
            for i, block in blocks.items():
                product = tap * block
                acc[b][i] = product if acc[b][i] is None else acc[b][i] + product
    return acc


def moved_sum(here, before, causal):
    row = lax.broadcasted_iota(jnp.int32, (TILE, LANES), 0)
    total = here[0]
    for b in range(1, TILE):
        if causal:
            picked = jnp.where(row < TILE - b, here[b], before[b])
            piece = pltpu.roll(picked, b, 0)
        else:
            picked = jnp.where(row >= b, here[b], before[b])
            piece = pltpu.roll(picked, TILE - b, 0)
        total = total + piece
    return total


def conv_local(source_ref, filters_ref, out_ref, causal):
    tiles = source_ref.shape[0] // TILE
    zero = jnp.zeros((TILE, LANES), F32)

    def row_of(u):
        return (u if causal else tiles - 1 - u) * TILE

    for lane_block in range(source_ref.shape[1] // LANES):
        lanes = slice(lane_block * LANES, (lane_block + 1) * LANES)

        def group(first, before, lanes, at):
            plan = [[(a, at(first + i - a)) for a in range(STEPS) if not isinstance(first, int) or first + i >= a] for i in range(GROUP)]
            acc = tap_sums(source_ref, filters_ref, lanes, plan)
            for i in range(GROUP):
                here = [acc[b][i] for b in range(TILE)]
                out_ref[pl.ds(at(first + i), TILE), lanes] = moved_sum(here, before, causal)
                before = here
            return before

        before = [zero] * TILE
        for g in range(STEPS // GROUP):
            before = group(g * GROUP, before, lanes, row_of)

        def step(g, carried, lanes=lanes, group=group):
            before = group(g * GROUP, [zero, *carried], lanes, lambda u: pl.multiple_of(row_of(u), TILE))
            return tuple(before[1:])

        lax.fori_loop(STEPS // GROUP, tiles // GROUP, step, tuple(before[1:]))


def conv_halo(source_ref, filters_ref, out_ref, causal):
    tiles = source_ref.shape[0] // TILE
    zero = jnp.zeros((TILE, LANES), F32)

    def row_of(u):
        return (u if causal else tiles - 1 - u) * TILE

    for lane_block in range(source_ref.shape[1] // LANES):
        lanes = slice(lane_block * LANES, (lane_block + 1) * LANES)
        before = [zero] * TILE
        for first in range(-1, tiles - 1, GROUP):
            plan = [[(a, row_of(tiles + u - a)) for a in range(u + 1, STEPS)] for u in range(first, first + GROUP)]
            acc = tap_sums(source_ref, filters_ref, lanes, plan)
            for i, u in enumerate(range(first, first + GROUP)):
                here = [acc[b][i] for b in range(TILE)]
                if u >= 0:
                    rows = slice(row_of(u), row_of(u) + TILE)
                    out_ref[rows, lanes] = out_ref[rows, lanes] + moved_sum(here, before, causal)
                before = here
        rows = slice(row_of(tiles - 1), row_of(tiles - 1) + TILE)
        out_ref[rows, lanes] = out_ref[rows, lanes] + moved_sum([zero] * TILE, before, causal)


def gate(query, conv_out):
    return (query.astype(F32) * conv_out).astype(BF16)


def blocks_after_far():
    return lax.axis_index("ctx") - lax.axis_size("ctx") // 2


def fore_early():
    after = blocks_after_far()
    return jnp.logical_and(after >= 0, after <= 1)


def back_early():
    return blocks_after_far() == 0


def ordered_chunks():
    place = lax.axis_index("tp")
    core = lax.rem(place, 2)
    chip = place // 2
    return [2 * at_chip + at_core for at_core in (core, 1 - core) for at_chip in (chip, 1 - chip)]


def inner_fore(operands, outs, query, source, conv):
    normed_ref, wq_ref, wk_ref, wv_ref, kvf_ref, filters_ref, wout_ref = operands
    q_ref, part_ref, term_ref, w_ref = outs
    half, width = kvf_ref.shape
    for part, number in enumerate(ordered_chunks()):
        w_ref[:, part * width : (part + 1) * width] = wout_ref[:, pl.ds(pl.multiple_of(number * width, width), width)]
    query[...] = dot(normed_ref[...], wq_ref[...]).astype(BF16)
    q_ref[...] = query[:half]
    source[:half] = keyval(normed_ref[:half], wk_ref, wv_ref).astype(F32)
    source[half:] = kvf_ref[...].astype(F32)
    conv_local(source, filters_ref, conv, True)
    part_ref[...] = conv[:half]
    term_ref[...] = dot(gate(query[half:], conv[half:]), w_ref[...])


def inner_back(operands, outs, query, source, conv, flipped):
    normed_ref, low_ref, wq_ref, wk_ref, wv_ref, kvb_ref, filters_ref, wout_ref, flip_ref = operands
    q_ref, part_ref, term_ref, w_ref = outs
    half, width = kvb_ref.shape
    for part, number in enumerate(ordered_chunks()):
        chunk = wout_ref[:, pl.ds(pl.multiple_of((3 - number) * width, width), width)]
        w_ref[:, part * width : (part + 1) * width] = dot(chunk, flip_ref[...]).astype(BF16)
    columns_reversed(normed_ref[half:], flip_ref[...], flipped)
    query[:half] = dot(low_ref[...], wq_ref[...]).astype(BF16)
    query[half:] = dot(flipped[...], wq_ref[...]).astype(BF16)
    q_ref[...] = query[half:]
    source[:half] = kvb_ref[...].astype(F32)
    source[half:] = keyval(flipped[...], wk_ref, wv_ref).astype(F32)
    conv_local(source, filters_ref, conv, False)
    part_ref[...] = conv[half:]
    term_ref[...] = dot(gate(query[:half], conv[:half]), w_ref[...])


INPUTS = 10


def strands(inputs, outs, scratch):
    normed_ref, low_ref, wq_ref, wk_ref, wv_ref, kvf_ref, kvb_ref, filters_ref, wout_ref, flip_ref = inputs
    fore = (normed_ref, wq_ref, wk_ref, wv_ref, kvf_ref, filters_ref, wout_ref)
    back = (normed_ref, low_ref, wq_ref, wk_ref, wv_ref, kvb_ref, filters_ref, wout_ref, flip_ref)
    return lambda: inner_fore(fore, outs[:4], *scratch[:3]), lambda: inner_back(back, outs[4:], *scratch)


def early_kernel(*refs):
    inputs, first_ref, rest = refs[:INPUTS], refs[INPUTS], refs[INPUTS + 1 :]
    fore, back = strands(inputs, rest[:8], rest[8:])
    first_ref[...] = inputs[6][...]
    pl.when(fore_early())(fore)
    pl.when(back_early())(back)


def inner_kernel(*refs):
    inputs, rest = refs[:INPUTS], refs[INPUTS:]
    early, outs, scratch = rest[:8], rest[8:16], rest[16:]
    fore, back = strands(inputs, outs, scratch)

    def copied(start):
        for i in range(start, start + 4):
            outs[i][...] = early[i][...]

    pl.when(fore_early())(lambda: copied(0))
    pl.when(back_early())(lambda: copied(4))
    pl.when(jnp.logical_not(fore_early()))(fore)
    pl.when(jnp.logical_not(back_early()))(back)


def outer(halo_ref, q_ref, part_ref, term_ref, w_ref, filters_ref, source, conv, causal):
    source[...] = halo_ref[...].astype(F32)
    conv[...] = part_ref[...]
    conv_halo(source, filters_ref, conv, causal)
    return term_ref[...] + dot(gate(q_ref[...], conv[...]), w_ref[...])


def fore_kernel(left_ref, qf_ref, pf_ref, tb_ref, wf_ref, filters_ref, keep_ref, send_ref, source, conv):
    width = keep_ref.shape[1]
    total = outer(left_ref, qf_ref, pf_ref, tb_ref, wf_ref, filters_ref, source, conv, True)
    keep_ref[...] = total[:, :width]
    send_ref[...] = total[:, width:].astype(BF16)


def back_kernel(right_ref, qb_ref, pb_ref, tf_ref, wb_ref, filters_ref, low_keep_ref, low_send_ref, keep_ref, send_ref, source, conv):
    half, width = low_keep_ref.shape
    total = outer(right_ref, qb_ref, pb_ref, tf_ref, wb_ref, filters_ref, source, conv, False)
    keep_ref[:half] = low_keep_ref[...]
    send_ref[:half] = low_send_ref[...]
    keep_ref[half:] = total[:, :width]
    send_ref[half:] = total[:, width:].astype(BF16)


def call(kernel, outs, scratch, flops, bytes_accessed, operands, in_hbm=()):
    vmem = pl.BlockSpec(memory_space=pltpu.VMEM)
    hbm = pl.BlockSpec(memory_space=pltpu.HBM)
    operands = [pltpu.with_memory_space_constraint(x, pltpu.HBM) if i in in_hbm else x for i, x in enumerate(operands)]
    return pl.pallas_call(
        kernel,
        out_shape=[jax.ShapeDtypeStruct(shape, kind) for shape, kind in outs],
        in_specs=[hbm if i in in_hbm else vmem for i in range(len(operands))],
        out_specs=[vmem] * len(outs),
        scratch_shapes=scratch,
        compiler_params=pltpu.CompilerParams(vmem_limit_bytes=32 * 1024 * 1024),
        cost_estimate=pl.CostEstimate(flops=flops, bytes_accessed=bytes_accessed, transcendentals=0),
    )(*operands)


def on_device(hidden, bases, base_table, norm_gain, w_query, w_key, w_value, w_out, filters):
    rows, channels = hidden.shape
    half = rows // 2
    width = w_query.shape[0]
    edge = ((half, channels), BF16)
    one_hot, flip = call(
        prepare_kernel,
        [((4, rows), BF16), ((channels, channels), BF16)],
        [pltpu.VMEM((1, rows), jnp.int32), pltpu.SemaphoreType.DMA(())],
        1_000_000_000,
        1_000,
        (bases.reshape(1, rows),),
        in_hbm=(0,),
    )
    shared, one_hot, flip = lax.optimization_barrier((hidden, one_hot, flip))
    gathered = lax.all_gather(shared, "tp", axis=1, tiled=True)
    normed, flipped, kvf, kvb = call(
        project_kernel,
        [((rows, width), BF16), ((half, width), BF16), edge, edge],
        [],
        600_000_000,
        4_000_000,
        (gathered, one_hot, base_table, norm_gain.reshape(1, width), w_key, w_value, flip),
    )
    partial = ((half, channels), F32)
    term = ((half, width), F32)
    weight = ((channels, width), BF16)
    inner_outs = [edge, partial, term, weight] * 2
    scratch = [pltpu.VMEM((rows, channels), BF16), pltpu.VMEM((rows, channels), F32), pltpu.VMEM((rows, channels), F32), pltpu.VMEM((half, width), BF16)]
    operands = (normed, flipped, w_query, w_key, w_value, kvf, kvb, filters, w_out, flip)
    left = passed_along(kvf, "ctx", 1)
    first, *early = call(early_kernel, [edge] + inner_outs, scratch, 1_000_000, 300_000, operands)
    right = passed_along(first, "ctx", -1)
    qf, pf, tf, wf, qb, pb, tb, wb = call(inner_kernel, inner_outs, scratch, 600_000_000, 300_000, operands + tuple(early))
    scratch = [pltpu.VMEM((half, channels), F32), pltpu.VMEM((half, channels), F32)]
    low = call(
        fore_kernel,
        [((half, 2 * channels), F32), ((half, 2 * channels), BF16)],
        scratch,
        500_000_000,
        2_000_000,
        (left, qf, pf, tb, wf, filters),
    )
    keep, send = call(
        back_kernel,
        [((rows, 2 * channels), F32), ((rows, 2 * channels), BF16)],
        scratch,
        500_000_000,
        2_000_000,
        (right, qb, pb, tf, wb, filters, *low),
    )
    place = lax.axis_index("tp")
    pair = lax.all_gather(send, "tp", axis_index_groups=CHIP_PAIRS)
    summed = keep + jnp.where(place % 2 == 0, pair[1], pair[0]).astype(F32)
    both = lax.all_gather(summed[:, channels:].astype(BF16), "tp", axis_index_groups=CORE_PAIRS)
    received = jnp.where(place < 2, both[1], both[0]).astype(F32)
    return (hidden.astype(F32) + summed[:, :channels] + received).astype(BF16)


def solution(mesh):
    in_specs = (
        P("ctx", "tp"),
        P("ctx"),
        P(),
        P(),
        P(None, "tp"),
        P(None, "tp"),
        P(None, "tp"),
        P("tp", None),
        P(None, "tp"),
    )
    return jax.shard_map(on_device, mesh=mesh, in_specs=in_specs, out_specs=P("ctx", "tp"), check_vma=False)
```

```python
import jax
import jax.numpy as jnp
from jax import lax
from jax.experimental import pallas as pl
from jax.experimental.pallas import tpu as pltpu
from jax.sharding import PartitionSpec as P

K = 128
TILE = 8
STEPS = K // TILE
LANES = 128
GROUP = 4
F32 = jnp.float32
BF16 = jnp.bfloat16
CHIP_PAIRS = [[0, 1], [2, 3]]
CORE_PAIRS = [[0, 2], [1, 3]]


def passed_along(block, distance, receivers):
    return lax.ppermute(block, "ctx", [(i - distance, i) for i in receivers])


def anti_identity(size):
    rows = lax.broadcasted_iota(jnp.int32, (size, size), 0)
    columns = lax.broadcasted_iota(jnp.int32, (size, size), 1)
    return jnp.where(rows + columns == size - 1, 1.0, 0.0).astype(BF16)


def dot(left, right):
    return jnp.dot(left, right, preferred_element_type=F32)


def columns_reversed(block, flip, out_ref):
    width = flip.shape[0]
    parts = block.shape[1] // width
    for part in range(parts):
        source = block[:, (parts - 1 - part) * width : (parts - part) * width]
        out_ref[:, part * width : (part + 1) * width] = dot(source, flip).astype(BF16)


def keyval(source, wk_ref, wv_ref):
    key = dot(source, wk_ref[...]).astype(BF16).astype(F32)
    value = dot(source, wv_ref[...]).astype(BF16).astype(F32)
    return (key * value).astype(BF16)


def prepare_kernel(bases_hbm, one_hot_ref, flip_ref, bases_ref, arrived):
    copy = pltpu.make_async_copy(bases_hbm, bases_ref, arrived)
    copy.start()
    flip_ref[...] = anti_identity(flip_ref.shape[0])
    copy.wait()
    base_rows = lax.broadcasted_iota(jnp.int32, one_hot_ref.shape, 0)
    one_hot_ref[...] = jnp.where(base_rows == bases_ref[...], 1.0, 0.0).astype(BF16)


def project_kernel(x_ref, one_hot_ref, table_ref, gain_ref, wk_ref, wv_ref, flip_ref, normed_ref, flipped_ref, kvf_ref, kvb_ref):
    half = kvf_ref.shape[0]
    embedded = lax.dot_general(one_hot_ref[...], table_ref[...], (((0,), (0,)), ((), ())), preferred_element_type=F32)
    summed = x_ref[...].astype(F32) + embedded
    mean_square = jnp.mean(summed * summed, axis=1, keepdims=True)
    normed = (summed * lax.rsqrt(mean_square + 1e-06) * gain_ref[...]).astype(BF16)
    normed_ref[...] = normed
    columns_reversed(normed[:half], flip_ref[...], flipped_ref)
    kvf_ref[...] = keyval(normed[half:], wk_ref, wv_ref)
    kvb_ref[...] = keyval(flipped_ref[...], wk_ref, wv_ref)


def tap_sums(source_ref, filters_ref, lanes, plan):
    acc = [[None] * len(plan) for _ in range(TILE)]
    for a in range(STEPS):
        starts = {i: dict(pairs)[a] for i, pairs in enumerate(plan) if a in dict(pairs)}
        blocks = {i: source_ref[pl.ds(start, TILE), lanes] for i, start in starts.items()}
        for b in range(TILE) if starts else ():
            tap = filters_ref[a * TILE + b : a * TILE + b + 1, lanes]
            for i, block in blocks.items():
                product = tap * block
                acc[b][i] = product if acc[b][i] is None else acc[b][i] + product
    return acc


def moved_sum(here, before, causal):
    row = lax.broadcasted_iota(jnp.int32, (TILE, LANES), 0)
    total = here[0]
    for b in range(1, TILE):
        if causal:
            picked = jnp.where(row < TILE - b, here[b], before[b])
            piece = pltpu.roll(picked, b, 0)
        else:
            picked = jnp.where(row >= b, here[b], before[b])
            piece = pltpu.roll(picked, TILE - b, 0)
        total = total + piece
    return total


def conv_local(source_ref, filters_ref, out_ref, causal):
    tiles = source_ref.shape[0] // TILE
    zero = jnp.zeros((TILE, LANES), F32)

    def row_of(u):
        return (u if causal else tiles - 1 - u) * TILE

    for lane_block in range(source_ref.shape[1] // LANES):
        lanes = slice(lane_block * LANES, (lane_block + 1) * LANES)

        def group(first, before, lanes, at):
            plan = [[(a, at(first + i - a)) for a in range(STEPS) if not isinstance(first, int) or first + i >= a] for i in range(GROUP)]
            acc = tap_sums(source_ref, filters_ref, lanes, plan)
            for i in range(GROUP):
                here = [acc[b][i] for b in range(TILE)]
                out_ref[pl.ds(at(first + i), TILE), lanes] = moved_sum(here, before, causal)
                before = here
            return before

        before = [zero] * TILE
        for g in range(STEPS // GROUP):
            before = group(g * GROUP, before, lanes, row_of)

        def step(g, carried, lanes=lanes, group=group):
            before = group(g * GROUP, [zero, *carried], lanes, lambda u: pl.multiple_of(row_of(u), TILE))
            return tuple(before[1:])

        lax.fori_loop(STEPS // GROUP, tiles // GROUP, step, tuple(before[1:]))


def conv_halo(source_ref, filters_ref, out_ref, causal):
    tiles = source_ref.shape[0] // TILE
    zero = jnp.zeros((TILE, LANES), F32)

    def row_of(u):
        return (u if causal else tiles - 1 - u) * TILE

    for lane_block in range(source_ref.shape[1] // LANES):
        lanes = slice(lane_block * LANES, (lane_block + 1) * LANES)
        before = [zero] * TILE
        for first in range(-1, tiles - 1, GROUP):
            plan = [[(a, row_of(tiles + u - a)) for a in range(u + 1, STEPS)] for u in range(first, first + GROUP)]
            acc = tap_sums(source_ref, filters_ref, lanes, plan)
            for i, u in enumerate(range(first, first + GROUP)):
                here = [acc[b][i] for b in range(TILE)]
                if u >= 0:
                    rows = slice(row_of(u), row_of(u) + TILE)
                    out_ref[rows, lanes] = out_ref[rows, lanes] + moved_sum(here, before, causal)
                before = here
        rows = slice(row_of(tiles - 1), row_of(tiles - 1) + TILE)
        out_ref[rows, lanes] = out_ref[rows, lanes] + moved_sum([zero] * TILE, before, causal)


def gate(query, conv_out):
    return (query.astype(F32) * conv_out).astype(BF16)


def blocks_after_far():
    return lax.axis_index("ctx") - lax.axis_size("ctx") // 2


def fore_early():
    after = blocks_after_far()
    return jnp.logical_and(after >= 0, after <= 1)


def back_early():
    return blocks_after_far() == 0


def ordered_chunks():
    place = lax.axis_index("tp")
    core = lax.rem(place, 2)
    chip = place // 2
    return [2 * at_chip + at_core for at_core in (core, 1 - core) for at_chip in (chip, 1 - chip)]


def inner_fore(operands, outs, query, source, conv):
    normed_ref, wq_ref, wk_ref, wv_ref, kvf_ref, filters_ref, wout_ref = operands
    q_ref, part_ref, term_ref, w_ref = outs
    half, width = kvf_ref.shape
    for part, number in enumerate(ordered_chunks()):
        w_ref[:, part * width : (part + 1) * width] = wout_ref[:, pl.ds(pl.multiple_of(number * width, width), width)]
    query[...] = dot(normed_ref[...], wq_ref[...]).astype(BF16)
    q_ref[...] = query[:half]
    source[:half] = keyval(normed_ref[:half], wk_ref, wv_ref).astype(F32)
    source[half:] = kvf_ref[...].astype(F32)
    conv_local(source, filters_ref, conv, True)
    part_ref[...] = conv[:half]
    term_ref[...] = dot(gate(query[half:], conv[half:]), w_ref[...])


def inner_back(operands, outs, query, source, conv, flipped):
    normed_ref, low_ref, wq_ref, wk_ref, wv_ref, kvb_ref, filters_ref, wout_ref, flip_ref = operands
    q_ref, part_ref, term_ref, w_ref = outs
    half, width = kvb_ref.shape
    for part, number in enumerate(ordered_chunks()):
        chunk = wout_ref[:, pl.ds(pl.multiple_of((3 - number) * width, width), width)]
        w_ref[:, part * width : (part + 1) * width] = dot(chunk, flip_ref[...]).astype(BF16)
    columns_reversed(normed_ref[half:], flip_ref[...], flipped)
    query[:half] = dot(low_ref[...], wq_ref[...]).astype(BF16)
    query[half:] = dot(flipped[...], wq_ref[...]).astype(BF16)
    q_ref[...] = query[half:]
    source[:half] = kvb_ref[...].astype(F32)
    source[half:] = keyval(flipped[...], wk_ref, wv_ref).astype(F32)
    conv_local(source, filters_ref, conv, False)
    part_ref[...] = conv[half:]
    term_ref[...] = dot(gate(query[:half], conv[:half]), w_ref[...])


INPUTS = 10


def strands(inputs, outs, scratch):
    normed_ref, low_ref, wq_ref, wk_ref, wv_ref, kvf_ref, kvb_ref, filters_ref, wout_ref, flip_ref = inputs
    fore = (normed_ref, wq_ref, wk_ref, wv_ref, kvf_ref, filters_ref, wout_ref)
    back = (normed_ref, low_ref, wq_ref, wk_ref, wv_ref, kvb_ref, filters_ref, wout_ref, flip_ref)
    return lambda: inner_fore(fore, outs[:4], *scratch[:3]), lambda: inner_back(back, outs[4:], *scratch)


def early_kernel(*refs):
    inputs, first_ref, last_ref, rest = refs[:INPUTS], refs[INPUTS], refs[INPUTS + 1], refs[INPUTS + 2 :]
    fore, back = strands(inputs, rest[:8], rest[8:])
    first_ref[...] = inputs[6][...]
    last_ref[...] = inputs[5][...]
    pl.when(fore_early())(fore)
    pl.when(back_early())(back)


def inner_kernel(*refs):
    inputs, rest = refs[:INPUTS], refs[INPUTS:]
    early, outs, scratch = rest[:8], rest[8:16], rest[16:]
    fore, back = strands(inputs, outs, scratch)

    def copied(start):
        for i in range(start, start + 4):
            outs[i][...] = early[i][...]

    pl.when(fore_early())(lambda: copied(0))
    pl.when(back_early())(lambda: copied(4))
    pl.when(jnp.logical_not(fore_early()))(fore)
    pl.when(jnp.logical_not(back_early()))(back)


def outer(halo_ref, q_ref, part_ref, term_ref, w_ref, filters_ref, source, conv, causal):
    source[...] = halo_ref[...].astype(F32)
    conv[...] = part_ref[...]
    conv_halo(source, filters_ref, conv, causal)
    return term_ref[...] + dot(gate(q_ref[...], conv[...]), w_ref[...])


def fore(left_ref, qf_ref, pf_ref, tb_ref, wf_ref, filters_ref, keep_ref, send_ref, source, conv):
    half = left_ref.shape[0]
    width = keep_ref.shape[1]
    total = outer(left_ref, qf_ref, pf_ref, tb_ref, wf_ref, filters_ref, source, conv, True)
    keep_ref[:half] = total[:, :width]
    send_ref[:half] = total[:, width:].astype(BF16)


def before_far():
    return blocks_after_far() == -1


def fore_kernel(*refs):
    @pl.when(jnp.logical_not(before_far()))
    def _():
        fore(*refs)


def back_kernel(right_ref, qb_ref, pb_ref, tf_ref, wb_ref, late_ref, qf_ref, pf_ref, tb_ref, wf_ref, filters_ref, low_keep_ref, low_send_ref, keep_ref, send_ref, source, conv):
    half, width = low_keep_ref.shape

    @pl.when(before_far())
    def _():
        fore(late_ref, qf_ref, pf_ref, tb_ref, wf_ref, filters_ref, keep_ref, send_ref, source, conv)

    @pl.when(jnp.logical_not(before_far()))
    def _():
        keep_ref[:half] = low_keep_ref[...]
        send_ref[:half] = low_send_ref[...]

    total = outer(right_ref, qb_ref, pb_ref, tf_ref, wb_ref, filters_ref, source, conv, False)
    keep_ref[half:] = total[:, :width]
    send_ref[half:] = total[:, width:].astype(BF16)


def call(kernel, outs, scratch, flops, bytes_accessed, operands, in_hbm=()):
    vmem = pl.BlockSpec(memory_space=pltpu.VMEM)
    hbm = pl.BlockSpec(memory_space=pltpu.HBM)
    operands = [pltpu.with_memory_space_constraint(x, pltpu.HBM) if i in in_hbm else x for i, x in enumerate(operands)]
    return pl.pallas_call(
        kernel,
        out_shape=[jax.ShapeDtypeStruct(shape, kind) for shape, kind in outs],
        in_specs=[hbm if i in in_hbm else vmem for i in range(len(operands))],
        out_specs=[vmem] * len(outs),
        scratch_shapes=scratch,
        compiler_params=pltpu.CompilerParams(vmem_limit_bytes=32 * 1024 * 1024),
        cost_estimate=pl.CostEstimate(flops=flops, bytes_accessed=bytes_accessed, transcendentals=0),
    )(*operands)


def on_device(hidden, bases, base_table, norm_gain, w_query, w_key, w_value, w_out, filters):
    rows, channels = hidden.shape
    half = rows // 2
    width = w_query.shape[0]
    edge = ((half, channels), BF16)
    one_hot, flip = call(
        prepare_kernel,
        [((4, rows), BF16), ((channels, channels), BF16)],
        [pltpu.VMEM((1, rows), jnp.int32), pltpu.SemaphoreType.DMA(())],
        1_000_000_000,
        1_000,
        (bases.reshape(1, rows),),
        in_hbm=(0,),
    )
    shared, one_hot, flip = lax.optimization_barrier((hidden, one_hot, flip))
    gathered = lax.all_gather(shared, "tp", axis=1, tiled=True)
    normed, flipped, kvf, kvb = call(
        project_kernel,
        [((rows, width), BF16), ((half, width), BF16), edge, edge],
        [],
        600_000_000,
        4_000_000,
        (gathered, one_hot, base_table, norm_gain.reshape(1, width), w_key, w_value, flip),
    )
    partial = ((half, channels), F32)
    term = ((half, width), F32)
    weight = ((channels, width), BF16)
    inner_outs = [edge, partial, term, weight] * 2
    scratch = [pltpu.VMEM((rows, channels), BF16), pltpu.VMEM((rows, channels), F32), pltpu.VMEM((rows, channels), F32), pltpu.VMEM((half, width), BF16)]
    operands = (normed, flipped, w_query, w_key, w_value, kvf, kvb, filters, w_out, flip)
    blocks = lax.axis_size("ctx")
    last_near = blocks // 2 - 1
    left = passed_along(kvf, 1, [i for i in range(1, blocks) if i != last_near])
    first, last, *early = call(early_kernel, [edge, edge] + inner_outs, scratch, 1_000_000, 300_000, operands)
    right = passed_along(first, -1, range(blocks - 1))
    late_left = passed_along(last, 1, [last_near])
    qf, pf, tf, wf, qb, pb, tb, wb = call(inner_kernel, inner_outs, scratch, 600_000_000, 300_000, operands + tuple(early))
    scratch = [pltpu.VMEM((half, channels), F32), pltpu.VMEM((half, channels), F32)]
    low = call(
        fore_kernel,
        [((half, 2 * channels), F32), ((half, 2 * channels), BF16)],
        scratch,
        500_000_000,
        2_000_000,
        (left, qf, pf, tb, wf, filters),
    )
    keep, send = call(
        back_kernel,
        [((rows, 2 * channels), F32), ((rows, 2 * channels), BF16)],
        scratch,
        500_000_000,
        2_000_000,
        (right, qb, pb, tf, wb, late_left, qf, pf, tb, wf, filters, *low),
    )
    place = lax.axis_index("tp")
    pair = lax.all_gather(send, "tp", axis_index_groups=CHIP_PAIRS)
    summed = keep + jnp.where(place % 2 == 0, pair[1], pair[0]).astype(F32)
    both = lax.all_gather(summed[:, channels:].astype(BF16), "tp", axis_index_groups=CORE_PAIRS)
    received = jnp.where(place < 2, both[1], both[0]).astype(F32)
    return (hidden.astype(F32) + summed[:, :channels] + received).astype(BF16)


def solution(mesh):
    in_specs = (
        P("ctx", "tp"),
        P("ctx"),
        P(),
        P(),
        P(None, "tp"),
        P(None, "tp"),
        P(None, "tp"),
        P("tp", None),
        P(None, "tp"),
    )
    return jax.shard_map(on_device, mesh=mesh, in_specs=in_specs, out_specs=P("ctx", "tp"), check_vma=False)
```

```python
import jax
import jax.numpy as jnp
from jax import lax
from jax.experimental import pallas as pl
from jax.experimental.pallas import tpu as pltpu
from jax.sharding import PartitionSpec as P

K = 128
TILE = 8
STEPS = K // TILE
LANES = 128
GROUP = 4
F32 = jnp.float32
BF16 = jnp.bfloat16
CHIP_PAIRS = [[0, 1], [2, 3]]
CORE_PAIRS = [[0, 2], [1, 3]]


def passed_along(block, distance, receivers):
    return lax.ppermute(block, "ctx", [(i - distance, i) for i in receivers])


def anti_identity(size):
    rows = lax.broadcasted_iota(jnp.int32, (size, size), 0)
    columns = lax.broadcasted_iota(jnp.int32, (size, size), 1)
    return jnp.where(rows + columns == size - 1, 1.0, 0.0).astype(BF16)


def dot(left, right):
    return jnp.dot(left, right, preferred_element_type=F32)


def columns_reversed(block, flip, out_ref):
    width = flip.shape[0]
    parts = block.shape[1] // width
    for part in range(parts):
        source = block[:, (parts - 1 - part) * width : (parts - part) * width]
        out_ref[:, part * width : (part + 1) * width] = dot(source, flip).astype(BF16)


def keyval(source, wk_ref, wv_ref):
    key = dot(source, wk_ref[...]).astype(BF16).astype(F32)
    value = dot(source, wv_ref[...]).astype(BF16).astype(F32)
    return (key * value).astype(BF16)


def prepare_kernel(bases_hbm, one_hot_ref, flip_ref, bases_ref, arrived):
    copy = pltpu.make_async_copy(bases_hbm, bases_ref, arrived)
    copy.start()
    flip_ref[...] = anti_identity(flip_ref.shape[0])
    copy.wait()
    base_rows = lax.broadcasted_iota(jnp.int32, one_hot_ref.shape, 0)
    one_hot_ref[...] = jnp.where(base_rows == bases_ref[...], 1.0, 0.0).astype(BF16)


def project_kernel(x_ref, one_hot_ref, table_ref, gain_ref, wk_ref, wv_ref, flip_ref, normed_ref, flipped_ref, kvf_ref, kvb_ref):
    half = kvf_ref.shape[0]
    embedded = lax.dot_general(one_hot_ref[...], table_ref[...], (((0,), (0,)), ((), ())), preferred_element_type=F32)
    summed = x_ref[...].astype(F32) + embedded
    mean_square = jnp.mean(summed * summed, axis=1, keepdims=True)
    normed = (summed * lax.rsqrt(mean_square + 1e-06) * gain_ref[...]).astype(BF16)
    normed_ref[...] = normed
    columns_reversed(normed[:half], flip_ref[...], flipped_ref)
    kvf_ref[...] = keyval(normed[half:], wk_ref, wv_ref)
    kvb_ref[...] = keyval(flipped_ref[...], wk_ref, wv_ref)


def tap_sums(source_ref, filters_ref, lanes, plan):
    acc = [[None] * len(plan) for _ in range(TILE)]
    for a in range(STEPS):
        starts = {i: dict(pairs)[a] for i, pairs in enumerate(plan) if a in dict(pairs)}
        blocks = {i: source_ref[pl.ds(start, TILE), lanes] for i, start in starts.items()}
        for b in range(TILE) if starts else ():
            tap = filters_ref[a * TILE + b : a * TILE + b + 1, lanes]
            for i, block in blocks.items():
                product = tap * block
                acc[b][i] = product if acc[b][i] is None else acc[b][i] + product
    return acc


def moved_sum(here, before, causal):
    row = lax.broadcasted_iota(jnp.int32, (TILE, LANES), 0)
    total = here[0]
    for b in range(1, TILE):
        if causal:
            picked = jnp.where(row < TILE - b, here[b], before[b])
            piece = pltpu.roll(picked, b, 0)
        else:
            picked = jnp.where(row >= b, here[b], before[b])
            piece = pltpu.roll(picked, TILE - b, 0)
        total = total + piece
    return total


def conv_local(source_ref, filters_ref, out_ref, causal):
    tiles = source_ref.shape[0] // TILE
    zero = jnp.zeros((TILE, LANES), F32)

    def row_of(u):
        return (u if causal else tiles - 1 - u) * TILE

    for lane_block in range(source_ref.shape[1] // LANES):
        lanes = slice(lane_block * LANES, (lane_block + 1) * LANES)

        def group(first, before, lanes, at):
            plan = [[(a, at(first + i - a)) for a in range(STEPS) if not isinstance(first, int) or first + i >= a] for i in range(GROUP)]
            acc = tap_sums(source_ref, filters_ref, lanes, plan)
            for i in range(GROUP):
                here = [acc[b][i] for b in range(TILE)]
                out_ref[pl.ds(at(first + i), TILE), lanes] = moved_sum(here, before, causal)
                before = here
            return before

        before = [zero] * TILE
        for g in range(STEPS // GROUP):
            before = group(g * GROUP, before, lanes, row_of)

        def step(g, carried, lanes=lanes, group=group):
            before = group(g * GROUP, [zero, *carried], lanes, lambda u: pl.multiple_of(row_of(u), TILE))
            return tuple(before[1:])

        lax.fori_loop(STEPS // GROUP, tiles // GROUP, step, tuple(before[1:]))


def conv_halo(source_ref, filters_ref, out_ref, causal):
    tiles = source_ref.shape[0] // TILE
    zero = jnp.zeros((TILE, LANES), F32)

    def row_of(u):
        return (u if causal else tiles - 1 - u) * TILE

    for lane_block in range(source_ref.shape[1] // LANES):
        lanes = slice(lane_block * LANES, (lane_block + 1) * LANES)
        before = [zero] * TILE
        for first in range(-1, tiles - 1, GROUP):
            plan = [[(a, row_of(tiles + u - a)) for a in range(u + 1, STEPS)] for u in range(first, first + GROUP)]
            acc = tap_sums(source_ref, filters_ref, lanes, plan)
            for i, u in enumerate(range(first, first + GROUP)):
                here = [acc[b][i] for b in range(TILE)]
                if u >= 0:
                    rows = slice(row_of(u), row_of(u) + TILE)
                    out_ref[rows, lanes] = out_ref[rows, lanes] + moved_sum(here, before, causal)
                before = here
        rows = slice(row_of(tiles - 1), row_of(tiles - 1) + TILE)
        out_ref[rows, lanes] = out_ref[rows, lanes] + moved_sum([zero] * TILE, before, causal)


def gate(query, conv_out):
    return (query.astype(F32) * conv_out).astype(BF16)


def blocks_after_far():
    return lax.axis_index("ctx") - lax.axis_size("ctx") // 2


def fore_early():
    after = blocks_after_far()
    return jnp.logical_and(after >= 0, after <= 1)


def back_early():
    return blocks_after_far() == 0


def ordered_chunks():
    place = lax.axis_index("tp")
    core = lax.rem(place, 2)
    chip = place // 2
    return [2 * at_chip + at_core for at_core in (core, 1 - core) for at_chip in (chip, 1 - chip)]


def inner_fore(operands, outs, query, source, conv):
    normed_ref, wq_ref, wk_ref, wv_ref, kvf_ref, filters_ref, wout_ref = operands
    q_ref, part_ref, term_ref, w_ref = outs
    half, width = kvf_ref.shape
    for part, number in enumerate(ordered_chunks()):
        w_ref[:, part * width : (part + 1) * width] = wout_ref[:, pl.ds(pl.multiple_of(number * width, width), width)]
    query[...] = dot(normed_ref[...], wq_ref[...]).astype(BF16)
    q_ref[...] = query[:half]
    source[:half] = keyval(normed_ref[:half], wk_ref, wv_ref).astype(F32)
    source[half:] = kvf_ref[...].astype(F32)
    conv_local(source, filters_ref, conv, True)
    part_ref[...] = conv[:half]
    term_ref[...] = dot(gate(query[half:], conv[half:]), w_ref[...])


def inner_back(operands, outs, query, source, conv, flipped):
    normed_ref, low_ref, wq_ref, wk_ref, wv_ref, kvb_ref, filters_ref, wout_ref, flip_ref = operands
    q_ref, part_ref, term_ref, w_ref = outs
    half, width = kvb_ref.shape
    for part, number in enumerate(ordered_chunks()):
        chunk = wout_ref[:, pl.ds(pl.multiple_of((3 - number) * width, width), width)]
        w_ref[:, part * width : (part + 1) * width] = dot(chunk, flip_ref[...]).astype(BF16)
    columns_reversed(normed_ref[half:], flip_ref[...], flipped)
    query[:half] = dot(low_ref[...], wq_ref[...]).astype(BF16)
    query[half:] = dot(flipped[...], wq_ref[...]).astype(BF16)
    q_ref[...] = query[half:]
    source[:half] = kvb_ref[...].astype(F32)
    source[half:] = keyval(flipped[...], wk_ref, wv_ref).astype(F32)
    conv_local(source, filters_ref, conv, False)
    part_ref[...] = conv[half:]
    term_ref[...] = dot(gate(query[:half], conv[:half]), w_ref[...])


INPUTS = 10


def strands(inputs, outs, scratch):
    normed_ref, low_ref, wq_ref, wk_ref, wv_ref, kvf_ref, kvb_ref, filters_ref, wout_ref, flip_ref = inputs
    fore = (normed_ref, wq_ref, wk_ref, wv_ref, kvf_ref, filters_ref, wout_ref)
    back = (normed_ref, low_ref, wq_ref, wk_ref, wv_ref, kvb_ref, filters_ref, wout_ref, flip_ref)
    return lambda: inner_fore(fore, outs[:4], *scratch[:3]), lambda: inner_back(back, outs[4:], *scratch)


def early_kernel(*refs):
    inputs, first_ref, last_ref, rest = refs[:INPUTS], refs[INPUTS], refs[INPUTS + 1], refs[INPUTS + 2 :]
    fore, back = strands(inputs, rest[:8], rest[8:])
    first_ref[...] = inputs[6][...]
    last_ref[...] = inputs[5][...]
    pl.when(fore_early())(fore)
    pl.when(back_early())(back)


def inner_kernel(*refs):
    inputs, rest = refs[:INPUTS], refs[INPUTS:]
    early, outs, scratch = rest[:8], rest[8:16], rest[16:]
    fore, back = strands(inputs, outs, scratch)

    def copied(start):
        for i in range(start, start + 4):
            outs[i][...] = early[i][...]

    pl.when(fore_early())(lambda: copied(0))
    pl.when(back_early())(lambda: copied(4))
    pl.when(jnp.logical_not(fore_early()))(fore)
    pl.when(jnp.logical_not(back_early()))(back)


def outer(halo_ref, q_ref, part_ref, filters_ref, source, conv, causal):
    source[...] = halo_ref[...].astype(F32)
    conv[...] = part_ref[...]
    conv_halo(source, filters_ref, conv, causal)
    return gate(q_ref[...], conv[...])


def before_far():
    return blocks_after_far() == -1


def fore_kernel(left_ref, qf_ref, pf_ref, filters_ref, mixed_ref, source, conv):
    @pl.when(jnp.logical_not(before_far()))
    def _():
        mixed_ref[...] = outer(left_ref, qf_ref, pf_ref, filters_ref, source, conv, True)


def back_kernel(right_ref, qb_ref, pb_ref, tf_ref, wb_ref, late_ref, qf_ref, pf_ref, tb_ref, wf_ref, filters_ref, low_ref, keep_ref, send_ref, source, conv, mixed):
    half, width = keep_ref.shape[0] // 2, keep_ref.shape[1]

    @pl.when(before_far())
    def _():
        mixed[...] = outer(late_ref, qf_ref, pf_ref, filters_ref, source, conv, True)

    @pl.when(jnp.logical_not(before_far()))
    def _():
        mixed[...] = low_ref[...]

    low = tb_ref[...] + dot(mixed[...], wf_ref[...])
    keep_ref[:half] = low[:, :width]
    send_ref[:half] = low[:, width:].astype(BF16)
    high = tf_ref[...] + dot(outer(right_ref, qb_ref, pb_ref, filters_ref, source, conv, False), wb_ref[...])
    keep_ref[half:] = high[:, :width]
    send_ref[half:] = high[:, width:].astype(BF16)


def call(kernel, outs, scratch, flops, bytes_accessed, operands, in_hbm=()):
    vmem = pl.BlockSpec(memory_space=pltpu.VMEM)
    hbm = pl.BlockSpec(memory_space=pltpu.HBM)
    operands = [pltpu.with_memory_space_constraint(x, pltpu.HBM) if i in in_hbm else x for i, x in enumerate(operands)]
    return pl.pallas_call(
        kernel,
        out_shape=[jax.ShapeDtypeStruct(shape, kind) for shape, kind in outs],
        in_specs=[hbm if i in in_hbm else vmem for i in range(len(operands))],
        out_specs=[vmem] * len(outs),
        scratch_shapes=scratch,
        compiler_params=pltpu.CompilerParams(vmem_limit_bytes=32 * 1024 * 1024),
        cost_estimate=pl.CostEstimate(flops=flops, bytes_accessed=bytes_accessed, transcendentals=0),
    )(*operands)


def on_device(hidden, bases, base_table, norm_gain, w_query, w_key, w_value, w_out, filters):
    rows, channels = hidden.shape
    half = rows // 2
    width = w_query.shape[0]
    edge = ((half, channels), BF16)
    one_hot, flip = call(
        prepare_kernel,
        [((4, rows), BF16), ((channels, channels), BF16)],
        [pltpu.VMEM((1, rows), jnp.int32), pltpu.SemaphoreType.DMA(())],
        1_000_000_000,
        1_000,
        (bases.reshape(1, rows),),
        in_hbm=(0,),
    )
    shared, one_hot, flip = lax.optimization_barrier((hidden, one_hot, flip))
    gathered = lax.all_gather(shared, "tp", axis=1, tiled=True)
    normed, flipped, kvf, kvb = call(
        project_kernel,
        [((rows, width), BF16), ((half, width), BF16), edge, edge],
        [],
        600_000_000,
        4_000_000,
        (gathered, one_hot, base_table, norm_gain.reshape(1, width), w_key, w_value, flip),
    )
    partial = ((half, channels), F32)
    term = ((half, width), F32)
    weight = ((channels, width), BF16)
    inner_outs = [edge, partial, term, weight] * 2
    scratch = [pltpu.VMEM((rows, channels), BF16), pltpu.VMEM((rows, channels), F32), pltpu.VMEM((rows, channels), F32), pltpu.VMEM((half, width), BF16)]
    operands = (normed, flipped, w_query, w_key, w_value, kvf, kvb, filters, w_out, flip)
    blocks = lax.axis_size("ctx")
    last_near = blocks // 2 - 1
    left = passed_along(kvf, 1, [i for i in range(1, blocks) if i != last_near])
    first, last, *early = call(early_kernel, [edge, edge] + inner_outs, scratch, 1_000_000, 300_000, operands)
    right = passed_along(first, -1, range(blocks - 1))
    late_left = passed_along(last, 1, [last_near])
    qf, pf, tf, wf, qb, pb, tb, wb = call(inner_kernel, inner_outs, scratch, 600_000_000, 300_000, operands + tuple(early))
    scratch = [pltpu.VMEM((half, channels), F32), pltpu.VMEM((half, channels), F32)]
    (low,) = call(fore_kernel, [edge], scratch, 500_000_000, 2_000_000, (left, qf, pf, filters))
    keep, send = call(
        back_kernel,
        [((rows, 2 * channels), F32), ((rows, 2 * channels), BF16)],
        scratch + [pltpu.VMEM((half, channels), BF16)],
        500_000_000,
        2_000_000,
        (right, qb, pb, tf, wb, late_left, qf, pf, tb, wf, filters, low),
    )
    place = lax.axis_index("tp")
    pair = lax.all_gather(send, "tp", axis_index_groups=CHIP_PAIRS)
    summed = keep + jnp.where(place % 2 == 0, pair[1], pair[0]).astype(F32)
    both = lax.all_gather(summed[:, channels:].astype(BF16), "tp", axis_index_groups=CORE_PAIRS)
    received = jnp.where(place < 2, both[1], both[0]).astype(F32)
    return (hidden.astype(F32) + summed[:, :channels] + received).astype(BF16)


def solution(mesh):
    in_specs = (
        P("ctx", "tp"),
        P("ctx"),
        P(),
        P(),
        P(None, "tp"),
        P(None, "tp"),
        P(None, "tp"),
        P("tp", None),
        P(None, "tp"),
    )
    return jax.shard_map(on_device, mesh=mesh, in_specs=in_specs, out_specs=P("ctx", "tp"), check_vma=False)
```

```python
import jax
import jax.numpy as jnp
from jax import lax
from jax.experimental import pallas as pl
from jax.experimental.pallas import tpu as pltpu
from jax.sharding import PartitionSpec as P

K = 128
TILE = 8
STEPS = K // TILE
LANES = 128
GROUP = 4
F32 = jnp.float32
BF16 = jnp.bfloat16
CHIP_PAIRS = [[0, 1], [2, 3]]
CORE_PAIRS = [[0, 2], [1, 3]]


def passed_along(block, distance, receivers):
    return lax.ppermute(block, "ctx", [(i - distance, i) for i in receivers])


def anti_identity(size):
    rows = lax.broadcasted_iota(jnp.int32, (size, size), 0)
    columns = lax.broadcasted_iota(jnp.int32, (size, size), 1)
    return jnp.where(rows + columns == size - 1, 1.0, 0.0).astype(BF16)


def dot(left, right):
    return jnp.dot(left, right, preferred_element_type=F32)


def columns_reversed(block, flip, out_ref):
    width = flip.shape[0]
    parts = block.shape[1] // width
    for part in range(parts):
        source = block[:, (parts - 1 - part) * width : (parts - part) * width]
        out_ref[:, part * width : (part + 1) * width] = dot(source, flip).astype(BF16)


def project(source, scale, w_ref):
    return (dot(source, w_ref[...]) * scale).astype(BF16)


def keyval(source, scale, wk_ref, wv_ref):
    key = project(source, scale, wk_ref).astype(F32)
    value = project(source, scale, wv_ref).astype(F32)
    return (key * value).astype(BF16)


def prepare_kernel(bases_hbm, one_hot_ref, flip_ref, bases_ref, arrived):
    copy = pltpu.make_async_copy(bases_hbm, bases_ref, arrived)
    copy.start()
    flip_ref[...] = anti_identity(flip_ref.shape[0])
    copy.wait()
    base_rows = lax.broadcasted_iota(jnp.int32, one_hot_ref.shape, 0)
    one_hot_ref[...] = jnp.where(base_rows == bases_ref[...], 1.0, 0.0).astype(BF16)


def project_kernel(x_ref, one_hot_ref, table_ref, gain_ref, wk_ref, wv_ref, flip_ref, gained_ref, flipped_ref, scale_ref, kvf_ref, kvb_ref):
    half = kvf_ref.shape[0]
    embedded = lax.dot_general(one_hot_ref[...], table_ref[...], (((0,), (0,)), ((), ())), preferred_element_type=F32)
    summed = x_ref[...].astype(F32) + embedded
    gained = (summed * gain_ref[...]).astype(BF16)
    gained_ref[...] = gained
    scale = lax.rsqrt(jnp.mean(summed * summed, axis=1, keepdims=True) + 1e-06)
    scale_ref[...] = scale
    columns_reversed(gained[:half], flip_ref[...], flipped_ref)
    kvf_ref[...] = keyval(gained[half:], scale[half:], wk_ref, wv_ref)
    kvb_ref[...] = keyval(flipped_ref[...], scale[:half], wk_ref, wv_ref)


def tap_sums(source_ref, filters_ref, lanes, plan):
    acc = [[None] * len(plan) for _ in range(TILE)]
    for a in range(STEPS):
        starts = {i: dict(pairs)[a] for i, pairs in enumerate(plan) if a in dict(pairs)}
        blocks = {i: source_ref[pl.ds(start, TILE), lanes] for i, start in starts.items()}
        for b in range(TILE) if starts else ():
            tap = filters_ref[a * TILE + b : a * TILE + b + 1, lanes]
            for i, block in blocks.items():
                product = tap * block
                acc[b][i] = product if acc[b][i] is None else acc[b][i] + product
    return acc


def moved_sum(here, before, causal):
    row = lax.broadcasted_iota(jnp.int32, (TILE, LANES), 0)
    total = here[0]
    for b in range(1, TILE):
        if causal:
            picked = jnp.where(row < TILE - b, here[b], before[b])
            piece = pltpu.roll(picked, b, 0)
        else:
            picked = jnp.where(row >= b, here[b], before[b])
            piece = pltpu.roll(picked, TILE - b, 0)
        total = total + piece
    return total


def conv_local(source_ref, filters_ref, out_ref, causal):
    tiles = source_ref.shape[0] // TILE
    zero = jnp.zeros((TILE, LANES), F32)

    def row_of(u):
        return (u if causal else tiles - 1 - u) * TILE

    for lane_block in range(source_ref.shape[1] // LANES):
        lanes = slice(lane_block * LANES, (lane_block + 1) * LANES)

        def group(first, before, lanes, at):
            plan = [[(a, at(first + i - a)) for a in range(STEPS) if not isinstance(first, int) or first + i >= a] for i in range(GROUP)]
            acc = tap_sums(source_ref, filters_ref, lanes, plan)
            for i in range(GROUP):
                here = [acc[b][i] for b in range(TILE)]
                out_ref[pl.ds(at(first + i), TILE), lanes] = moved_sum(here, before, causal)
                before = here
            return before

        before = [zero] * TILE
        for g in range(STEPS // GROUP):
            before = group(g * GROUP, before, lanes, row_of)

        def step(g, carried, lanes=lanes, group=group):
            before = group(g * GROUP, [zero, *carried], lanes, lambda u: pl.multiple_of(row_of(u), TILE))
            return tuple(before[1:])

        lax.fori_loop(STEPS // GROUP, tiles // GROUP, step, tuple(before[1:]))


def conv_halo(source_ref, filters_ref, out_ref, causal):
    tiles = source_ref.shape[0] // TILE
    zero = jnp.zeros((TILE, LANES), F32)

    def row_of(u):
        return (u if causal else tiles - 1 - u) * TILE

    for lane_block in range(source_ref.shape[1] // LANES):
        lanes = slice(lane_block * LANES, (lane_block + 1) * LANES)
        before = [zero] * TILE
        for first in range(-1, tiles - 1, GROUP):
            plan = [[(a, row_of(tiles + u - a)) for a in range(u + 1, STEPS)] for u in range(first, first + GROUP)]
            acc = tap_sums(source_ref, filters_ref, lanes, plan)
            for i, u in enumerate(range(first, first + GROUP)):
                here = [acc[b][i] for b in range(TILE)]
                if u >= 0:
                    rows = slice(row_of(u), row_of(u) + TILE)
                    out_ref[rows, lanes] = out_ref[rows, lanes] + moved_sum(here, before, causal)
                before = here
        rows = slice(row_of(tiles - 1), row_of(tiles - 1) + TILE)
        out_ref[rows, lanes] = out_ref[rows, lanes] + moved_sum([zero] * TILE, before, causal)


def gate(query, conv_out):
    return (query.astype(F32) * conv_out).astype(BF16)


def blocks_after_far():
    return lax.axis_index("ctx") - lax.axis_size("ctx") // 2


def fore_early():
    after = blocks_after_far()
    return jnp.logical_and(after >= 0, after <= 1)


def back_early():
    return blocks_after_far() == 0


def ordered_chunks():
    place = lax.axis_index("tp")
    core = lax.rem(place, 2)
    chip = place // 2
    return [2 * at_chip + at_core for at_core in (core, 1 - core) for at_chip in (chip, 1 - chip)]


def inner_fore(operands, outs, query, source, conv):
    gained_ref, scale_ref, wq_ref, wk_ref, wv_ref, kvf_ref, filters_ref, wout_ref = operands
    q_ref, part_ref, term_ref, w_ref = outs
    half, width = kvf_ref.shape
    for part, number in enumerate(ordered_chunks()):
        w_ref[:, part * width : (part + 1) * width] = wout_ref[:, pl.ds(pl.multiple_of(number * width, width), width)]
    query[...] = project(gained_ref[...], scale_ref[...], wq_ref)
    q_ref[...] = query[:half]
    source[:half] = keyval(gained_ref[:half], scale_ref[:half], wk_ref, wv_ref).astype(F32)
    source[half:] = kvf_ref[...].astype(F32)
    conv_local(source, filters_ref, conv, True)
    part_ref[...] = conv[:half]
    term_ref[...] = dot(gate(query[half:], conv[half:]), w_ref[...])


def inner_back(operands, outs, query, source, conv, flipped):
    gained_ref, low_ref, scale_ref, wq_ref, wk_ref, wv_ref, kvb_ref, filters_ref, wout_ref, flip_ref = operands
    q_ref, part_ref, term_ref, w_ref = outs
    half, width = kvb_ref.shape
    for part, number in enumerate(ordered_chunks()):
        chunk = wout_ref[:, pl.ds(pl.multiple_of((3 - number) * width, width), width)]
        w_ref[:, part * width : (part + 1) * width] = dot(chunk, flip_ref[...]).astype(BF16)
    columns_reversed(gained_ref[half:], flip_ref[...], flipped)
    query[:half] = project(low_ref[...], scale_ref[:half], wq_ref)
    query[half:] = project(flipped[...], scale_ref[half:], wq_ref)
    q_ref[...] = query[half:]
    source[:half] = kvb_ref[...].astype(F32)
    source[half:] = keyval(flipped[...], scale_ref[half:], wk_ref, wv_ref).astype(F32)
    conv_local(source, filters_ref, conv, False)
    part_ref[...] = conv[half:]
    term_ref[...] = dot(gate(query[:half], conv[:half]), w_ref[...])


INPUTS = 11


def strands(inputs, outs, scratch):
    gained_ref, low_ref, scale_ref, wq_ref, wk_ref, wv_ref, kvf_ref, kvb_ref, filters_ref, wout_ref, flip_ref = inputs
    fore = (gained_ref, scale_ref, wq_ref, wk_ref, wv_ref, kvf_ref, filters_ref, wout_ref)
    back = (gained_ref, low_ref, scale_ref, wq_ref, wk_ref, wv_ref, kvb_ref, filters_ref, wout_ref, flip_ref)
    return lambda: inner_fore(fore, outs[:4], *scratch[:3]), lambda: inner_back(back, outs[4:], *scratch)


def early_kernel(*refs):
    inputs, first_ref, last_ref, rest = refs[:INPUTS], refs[INPUTS], refs[INPUTS + 1], refs[INPUTS + 2 :]
    fore, back = strands(inputs, rest[:8], rest[8:])
    first_ref[...] = inputs[7][...]
    last_ref[...] = inputs[6][...]
    pl.when(fore_early())(fore)
    pl.when(back_early())(back)


def inner_kernel(*refs):
    inputs, rest = refs[:INPUTS], refs[INPUTS:]
    early, outs, scratch = rest[:8], rest[8:16], rest[16:]
    fore, back = strands(inputs, outs, scratch)

    def copied(start):
        for i in range(start, start + 4):
            outs[i][...] = early[i][...]

    pl.when(fore_early())(lambda: copied(0))
    pl.when(back_early())(lambda: copied(4))
    pl.when(jnp.logical_not(fore_early()))(fore)
    pl.when(jnp.logical_not(back_early()))(back)


def outer(halo_ref, q_ref, part_ref, term_ref, w_ref, filters_ref, source, conv, causal):
    source[...] = halo_ref[...].astype(F32)
    conv[...] = part_ref[...]
    conv_halo(source, filters_ref, conv, causal)
    return term_ref[...] + dot(gate(q_ref[...], conv[...]), w_ref[...])


def fore(left_ref, qf_ref, pf_ref, tb_ref, wf_ref, filters_ref, keep_ref, send_ref, source, conv):
    half = left_ref.shape[0]
    width = keep_ref.shape[1]
    total = outer(left_ref, qf_ref, pf_ref, tb_ref, wf_ref, filters_ref, source, conv, True)
    keep_ref[:half] = total[:, :width]
    send_ref[:half] = total[:, width:].astype(BF16)


def before_far():
    return blocks_after_far() == -1


def fore_kernel(*refs):
    @pl.when(jnp.logical_not(before_far()))
    def _():
        fore(*refs)


def back_kernel(right_ref, qb_ref, pb_ref, tf_ref, wb_ref, late_ref, qf_ref, pf_ref, tb_ref, wf_ref, filters_ref, low_keep_ref, low_send_ref, keep_ref, send_ref, source, conv):
    half, width = low_keep_ref.shape

    @pl.when(before_far())
    def _():
        fore(late_ref, qf_ref, pf_ref, tb_ref, wf_ref, filters_ref, keep_ref, send_ref, source, conv)

    @pl.when(jnp.logical_not(before_far()))
    def _():
        keep_ref[:half] = low_keep_ref[...]
        send_ref[:half] = low_send_ref[...]

    total = outer(right_ref, qb_ref, pb_ref, tf_ref, wb_ref, filters_ref, source, conv, False)
    keep_ref[half:] = total[:, :width]
    send_ref[half:] = total[:, width:].astype(BF16)


def call(kernel, outs, scratch, flops, bytes_accessed, operands, in_hbm=()):
    vmem = pl.BlockSpec(memory_space=pltpu.VMEM)
    hbm = pl.BlockSpec(memory_space=pltpu.HBM)
    operands = [pltpu.with_memory_space_constraint(x, pltpu.HBM) if i in in_hbm else x for i, x in enumerate(operands)]
    return pl.pallas_call(
        kernel,
        out_shape=[jax.ShapeDtypeStruct(shape, kind) for shape, kind in outs],
        in_specs=[hbm if i in in_hbm else vmem for i in range(len(operands))],
        out_specs=[vmem] * len(outs),
        scratch_shapes=scratch,
        compiler_params=pltpu.CompilerParams(vmem_limit_bytes=32 * 1024 * 1024),
        cost_estimate=pl.CostEstimate(flops=flops, bytes_accessed=bytes_accessed, transcendentals=0),
    )(*operands)


def on_device(hidden, bases, base_table, norm_gain, w_query, w_key, w_value, w_out, filters):
    rows, channels = hidden.shape
    half = rows // 2
    width = w_query.shape[0]
    edge = ((half, channels), BF16)
    one_hot, flip = call(
        prepare_kernel,
        [((4, rows), BF16), ((channels, channels), BF16)],
        [pltpu.VMEM((1, rows), jnp.int32), pltpu.SemaphoreType.DMA(())],
        1_000_000_000,
        1_000,
        (bases.reshape(1, rows),),
        in_hbm=(0,),
    )
    shared, one_hot, flip = lax.optimization_barrier((hidden, one_hot, flip))
    gathered = lax.all_gather(shared, "tp", axis=1, tiled=True)
    gained, flipped, scale, kvf, kvb = call(
        project_kernel,
        [((rows, width), BF16), ((half, width), BF16), ((rows, 1), F32), edge, edge],
        [],
        600_000_000,
        4_000_000,
        (gathered, one_hot, base_table, norm_gain.reshape(1, width), w_key, w_value, flip),
    )
    partial = ((half, channels), F32)
    term = ((half, width), F32)
    weight = ((channels, width), BF16)
    inner_outs = [edge, partial, term, weight] * 2
    scratch = [pltpu.VMEM((rows, channels), BF16), pltpu.VMEM((rows, channels), F32), pltpu.VMEM((rows, channels), F32), pltpu.VMEM((half, width), BF16)]
    operands = (gained, flipped, scale, w_query, w_key, w_value, kvf, kvb, filters, w_out, flip)
    blocks = lax.axis_size("ctx")
    last_near = blocks // 2 - 1
    left = passed_along(kvf, 1, [i for i in range(1, blocks) if i != last_near])
    first, last, *early = call(early_kernel, [edge, edge] + inner_outs, scratch, 1_000_000, 300_000, operands)
    right = passed_along(first, -1, range(blocks - 1))
    late_left = passed_along(last, 1, [last_near])
    qf, pf, tf, wf, qb, pb, tb, wb = call(inner_kernel, inner_outs, scratch, 600_000_000, 300_000, operands + tuple(early))
    scratch = [pltpu.VMEM((half, channels), F32), pltpu.VMEM((half, channels), F32)]
    low = call(
        fore_kernel,
        [((half, 2 * channels), F32), ((half, 2 * channels), BF16)],
        scratch,
        500_000_000,
        2_000_000,
        (left, qf, pf, tb, wf, filters),
    )
    keep, send = call(
        back_kernel,
        [((rows, 2 * channels), F32), ((rows, 2 * channels), BF16)],
        scratch,
        500_000_000,
        2_000_000,
        (right, qb, pb, tf, wb, late_left, qf, pf, tb, wf, filters, *low),
    )
    place = lax.axis_index("tp")
    pair = lax.all_gather(send, "tp", axis_index_groups=CHIP_PAIRS)
    summed = keep + jnp.where(place % 2 == 0, pair[1], pair[0]).astype(F32)
    both = lax.all_gather(summed[:, channels:].astype(BF16), "tp", axis_index_groups=CORE_PAIRS)
    received = jnp.where(place < 2, both[1], both[0]).astype(F32)
    return (hidden.astype(F32) + summed[:, :channels] + received).astype(BF16)


def solution(mesh):
    in_specs = (
        P("ctx", "tp"),
        P("ctx"),
        P(),
        P(),
        P(None, "tp"),
        P(None, "tp"),
        P(None, "tp"),
        P("tp", None),
        P(None, "tp"),
    )
    return jax.shard_map(on_device, mesh=mesh, in_specs=in_specs, out_specs=P("ctx", "tp"), check_vma=False)
```

```python
import jax
import jax.numpy as jnp
from jax import lax
from jax.experimental import pallas as pl
from jax.experimental.pallas import tpu as pltpu
from jax.sharding import PartitionSpec as P

K = 128
TILE = 8
STEPS = K // TILE
LANES = 128
GROUP = 4
F32 = jnp.float32
BF16 = jnp.bfloat16
CHIP_PAIRS = [[0, 1], [2, 3]]
CORE_PAIRS = [[0, 2], [1, 3]]


def passed_along(block, distance, receivers):
    return lax.ppermute(block, "ctx", [(i - distance, i) for i in receivers])


def anti_identity(size):
    rows = lax.broadcasted_iota(jnp.int32, (size, size), 0)
    columns = lax.broadcasted_iota(jnp.int32, (size, size), 1)
    return jnp.where(rows + columns == size - 1, 1.0, 0.0).astype(BF16)


def dot(left, right):
    return jnp.dot(left, right, preferred_element_type=F32)


def columns_reversed(block, flip, out_ref):
    width = flip.shape[0]
    parts = block.shape[1] // width
    for part in range(parts):
        source = block[:, (parts - 1 - part) * width : (parts - part) * width]
        out_ref[:, part * width : (part + 1) * width] = dot(source, flip).astype(BF16)


def project(source, scale, w_ref):
    return (dot(source, w_ref[...]) * scale).astype(BF16)


def keyval(source, scale, wk_ref, wv_ref):
    key = project(source, scale, wk_ref).astype(F32)
    value = project(source, scale, wv_ref).astype(F32)
    return (key * value).astype(BF16)


def prepare_kernel(bases_hbm, one_hot_ref, flip_ref, bases_ref, arrived):
    copy = pltpu.make_async_copy(bases_hbm, bases_ref, arrived)
    copy.start()
    flip_ref[...] = anti_identity(flip_ref.shape[0])
    copy.wait()
    base_rows = lax.broadcasted_iota(jnp.int32, one_hot_ref.shape, 0)
    one_hot_ref[...] = jnp.where(base_rows == bases_ref[...], 1.0, 0.0).astype(BF16)


def project_kernel(x_ref, one_hot_ref, table_ref, gain_ref, wk_ref, wv_ref, flip_ref, gained_ref, flipped_ref, scale_ref, kvf_ref, kvb_ref):
    half = kvf_ref.shape[0]
    embedded = lax.dot_general(one_hot_ref[...], table_ref[...], (((0,), (0,)), ((), ())), preferred_element_type=F32)
    summed = x_ref[...].astype(F32) + embedded
    gained = (summed * gain_ref[...]).astype(BF16)
    gained_ref[...] = gained
    scale = lax.rsqrt(jnp.mean(summed * summed, axis=1, keepdims=True) + 1e-06)
    scale_ref[...] = scale
    columns_reversed(gained[:half], flip_ref[...], flipped_ref)
    kvf_ref[...] = keyval(gained[half:], scale[half:], wk_ref, wv_ref)
    kvb_ref[...] = keyval(flipped_ref[...], scale[:half], wk_ref, wv_ref)


def tap_sums(source_ref, filters_ref, lanes, plan):
    acc = [[None] * len(plan) for _ in range(TILE)]
    for a in range(STEPS):
        starts = {i: dict(pairs)[a] for i, pairs in enumerate(plan) if a in dict(pairs)}
        blocks = {i: source_ref[pl.ds(start, TILE), lanes] for i, start in starts.items()}
        for b in range(TILE) if starts else ():
            tap = filters_ref[a * TILE + b : a * TILE + b + 1, lanes]
            for i, block in blocks.items():
                product = tap * block
                acc[b][i] = product if acc[b][i] is None else acc[b][i] + product
    return acc


def moved_sum(here, before, causal):
    row = lax.broadcasted_iota(jnp.int32, (TILE, LANES), 0)
    total = here[0]
    for b in range(1, TILE):
        if causal:
            picked = jnp.where(row < TILE - b, here[b], before[b])
            piece = pltpu.roll(picked, b, 0)
        else:
            picked = jnp.where(row >= b, here[b], before[b])
            piece = pltpu.roll(picked, TILE - b, 0)
        total = total + piece
    return total


def conv_local(source_ref, filters_ref, out_ref, causal):
    tiles = source_ref.shape[0] // TILE
    zero = jnp.zeros((TILE, LANES), F32)

    def row_of(u):
        return (u if causal else tiles - 1 - u) * TILE

    for lane_block in range(source_ref.shape[1] // LANES):
        lanes = slice(lane_block * LANES, (lane_block + 1) * LANES)

        def group(first, before, lanes, at):
            plan = [[(a, at(first + i - a)) for a in range(STEPS) if not isinstance(first, int) or first + i >= a] for i in range(GROUP)]
            acc = tap_sums(source_ref, filters_ref, lanes, plan)
            for i in range(GROUP):
                here = [acc[b][i] for b in range(TILE)]
                out_ref[pl.ds(at(first + i), TILE), lanes] = moved_sum(here, before, causal)
                before = here
            return before

        before = [zero] * TILE
        for g in range(STEPS // GROUP):
            before = group(g * GROUP, before, lanes, row_of)

        def step(g, carried, lanes=lanes, group=group):
            before = group(g * GROUP, [zero, *carried], lanes, lambda u: pl.multiple_of(row_of(u), TILE))
            return tuple(before[1:])

        lax.fori_loop(STEPS // GROUP, tiles // GROUP, step, tuple(before[1:]))


def conv_halo(source_ref, filters_ref, out_ref, causal):
    tiles = source_ref.shape[0] // TILE
    zero = jnp.zeros((TILE, LANES), F32)

    def row_of(u):
        return (u if causal else tiles - 1 - u) * TILE

    for lane_block in range(source_ref.shape[1] // LANES):
        lanes = slice(lane_block * LANES, (lane_block + 1) * LANES)
        before = [zero] * TILE
        for first in range(-1, tiles - 1, GROUP):
            plan = [[(a, row_of(tiles + u - a)) for a in range(u + 1, STEPS)] for u in range(first, first + GROUP)]
            acc = tap_sums(source_ref, filters_ref, lanes, plan)
            for i, u in enumerate(range(first, first + GROUP)):
                here = [acc[b][i] for b in range(TILE)]
                if u >= 0:
                    rows = slice(row_of(u), row_of(u) + TILE)
                    out_ref[rows, lanes] = out_ref[rows, lanes] + moved_sum(here, before, causal)
                before = here
        rows = slice(row_of(tiles - 1), row_of(tiles - 1) + TILE)
        out_ref[rows, lanes] = out_ref[rows, lanes] + moved_sum([zero] * TILE, before, causal)


def gate(query, conv_out):
    return (query.astype(F32) * conv_out).astype(BF16)


def blocks_after_far():
    return lax.axis_index("ctx") - lax.axis_size("ctx") // 2


def fore_early():
    after = blocks_after_far()
    return jnp.logical_and(after >= 0, after <= 1)


def back_early():
    return blocks_after_far() == 0


def ordered_chunks():
    place = lax.axis_index("tp")
    core = lax.rem(place, 2)
    chip = place // 2
    return [2 * at_chip + at_core for at_core in (core, 1 - core) for at_chip in (chip, 1 - chip)]


def inner_fore(operands, outs, query, source, conv):
    gained_ref, scale_ref, wq_ref, wk_ref, wv_ref, kvf_ref, filters_ref, wout_ref = operands
    q_ref, part_ref, term_ref, w_ref = outs
    half, width = kvf_ref.shape
    for part, number in enumerate(ordered_chunks()):
        w_ref[:, part * width : (part + 1) * width] = wout_ref[:, pl.ds(pl.multiple_of(number * width, width), width)]
    query[...] = project(gained_ref[...], scale_ref[...], wq_ref)
    q_ref[...] = query[:half]
    source[:half] = keyval(gained_ref[:half], scale_ref[:half], wk_ref, wv_ref).astype(F32)
    source[half:] = kvf_ref[...].astype(F32)
    conv_local(source, filters_ref, conv, True)
    part_ref[...] = conv[:half]
    term_ref[...] = dot(gate(query[half:], conv[half:]), w_ref[...])


def inner_back(operands, outs, query, source, conv, flipped):
    gained_ref, low_ref, scale_ref, wq_ref, wk_ref, wv_ref, kvb_ref, filters_ref, wout_ref, flip_ref = operands
    q_ref, part_ref, term_ref, w_ref = outs
    half, width = kvb_ref.shape
    for part, number in enumerate(ordered_chunks()):
        chunk = wout_ref[:, pl.ds(pl.multiple_of((3 - number) * width, width), width)]
        w_ref[:, part * width : (part + 1) * width] = dot(chunk, flip_ref[...]).astype(BF16)
    columns_reversed(gained_ref[half:], flip_ref[...], flipped)
    query[:half] = project(low_ref[...], scale_ref[:half], wq_ref)
    query[half:] = project(flipped[...], scale_ref[half:], wq_ref)
    q_ref[...] = query[half:]
    source[:half] = kvb_ref[...].astype(F32)
    source[half:] = keyval(flipped[...], scale_ref[half:], wk_ref, wv_ref).astype(F32)
    conv_local(source, filters_ref, conv, False)
    part_ref[...] = conv[half:]
    term_ref[...] = dot(gate(query[:half], conv[:half]), w_ref[...])


INPUTS = 11


def strands(inputs, outs, scratch):
    gained_ref, low_ref, scale_ref, wq_ref, wk_ref, wv_ref, kvf_ref, kvb_ref, filters_ref, wout_ref, flip_ref = inputs
    fore = (gained_ref, scale_ref, wq_ref, wk_ref, wv_ref, kvf_ref, filters_ref, wout_ref)
    back = (gained_ref, low_ref, scale_ref, wq_ref, wk_ref, wv_ref, kvb_ref, filters_ref, wout_ref, flip_ref)
    return lambda: inner_fore(fore, outs[:4], *scratch[:3]), lambda: inner_back(back, outs[4:], *scratch)


def early_kernel(*refs):
    inputs, first_ref, last_ref, rest = refs[:INPUTS], refs[INPUTS], refs[INPUTS + 1], refs[INPUTS + 2 :]
    fore, back = strands(inputs, rest[:8], rest[8:])
    first_ref[...] = inputs[7][...]
    last_ref[...] = inputs[6][...]
    pl.when(fore_early())(fore)
    pl.when(back_early())(back)


def inner_kernel(*refs):
    inputs, rest = refs[:INPUTS], refs[INPUTS:]
    early, outs, scratch = rest[:8], rest[8:16], rest[16:]
    fore, back = strands(inputs, outs, scratch)

    def copied(start):
        for i in range(start, start + 4):
            outs[i][...] = early[i][...]

    pl.when(fore_early())(lambda: copied(0))
    pl.when(back_early())(lambda: copied(4))
    pl.when(jnp.logical_not(fore_early()))(fore)
    pl.when(jnp.logical_not(back_early()))(back)


def outer(halo_ref, q_ref, part_ref, term_ref, w_ref, filters_ref, source, conv, causal):
    source[...] = halo_ref[...].astype(F32)
    conv[...] = part_ref[...]
    conv_halo(source, filters_ref, conv, causal)
    return term_ref[...] + dot(gate(q_ref[...], conv[...]), w_ref[...])


def fore(left_ref, qf_ref, pf_ref, tb_ref, wf_ref, filters_ref, keep_ref, send_ref, source, conv):
    half = left_ref.shape[0]
    width = keep_ref.shape[1]
    total = outer(left_ref, qf_ref, pf_ref, tb_ref, wf_ref, filters_ref, source, conv, True)
    keep_ref[:half] = total[:, :width].astype(BF16)
    send_ref[:half] = total[:, width:].astype(BF16)


def before_far():
    return blocks_after_far() == -1


def fore_kernel(*refs):
    @pl.when(jnp.logical_not(before_far()))
    def _():
        fore(*refs)


def back_kernel(right_ref, qb_ref, pb_ref, tf_ref, wb_ref, late_ref, qf_ref, pf_ref, tb_ref, wf_ref, filters_ref, low_keep_ref, low_send_ref, keep_ref, send_ref, source, conv):
    half, width = low_keep_ref.shape

    @pl.when(before_far())
    def _():
        fore(late_ref, qf_ref, pf_ref, tb_ref, wf_ref, filters_ref, keep_ref, send_ref, source, conv)

    @pl.when(jnp.logical_not(before_far()))
    def _():
        keep_ref[:half] = low_keep_ref[...]
        send_ref[:half] = low_send_ref[...]

    total = outer(right_ref, qb_ref, pb_ref, tf_ref, wb_ref, filters_ref, source, conv, False)
    keep_ref[half:] = total[:, :width].astype(BF16)
    send_ref[half:] = total[:, width:].astype(BF16)


def call(kernel, outs, scratch, flops, bytes_accessed, operands, in_hbm=()):
    vmem = pl.BlockSpec(memory_space=pltpu.VMEM)
    hbm = pl.BlockSpec(memory_space=pltpu.HBM)
    operands = [pltpu.with_memory_space_constraint(x, pltpu.HBM) if i in in_hbm else x for i, x in enumerate(operands)]
    return pl.pallas_call(
        kernel,
        out_shape=[jax.ShapeDtypeStruct(shape, kind) for shape, kind in outs],
        in_specs=[hbm if i in in_hbm else vmem for i in range(len(operands))],
        out_specs=[vmem] * len(outs),
        scratch_shapes=scratch,
        compiler_params=pltpu.CompilerParams(vmem_limit_bytes=32 * 1024 * 1024),
        cost_estimate=pl.CostEstimate(flops=flops, bytes_accessed=bytes_accessed, transcendentals=0),
    )(*operands)


def on_device(hidden, bases, base_table, norm_gain, w_query, w_key, w_value, w_out, filters):
    rows, channels = hidden.shape
    half = rows // 2
    width = w_query.shape[0]
    edge = ((half, channels), BF16)
    one_hot, flip = call(
        prepare_kernel,
        [((4, rows), BF16), ((channels, channels), BF16)],
        [pltpu.VMEM((1, rows), jnp.int32), pltpu.SemaphoreType.DMA(())],
        1_000_000_000,
        1_000,
        (bases.reshape(1, rows),),
        in_hbm=(0,),
    )
    shared, one_hot, flip = lax.optimization_barrier((hidden, one_hot, flip))
    gathered = lax.all_gather(shared, "tp", axis=1, tiled=True)
    gained, flipped, scale, kvf, kvb = call(
        project_kernel,
        [((rows, width), BF16), ((half, width), BF16), ((rows, 1), F32), edge, edge],
        [],
        600_000_000,
        4_000_000,
        (gathered, one_hot, base_table, norm_gain.reshape(1, width), w_key, w_value, flip),
    )
    partial = ((half, channels), F32)
    term = ((half, width), F32)
    weight = ((channels, width), BF16)
    inner_outs = [edge, partial, term, weight] * 2
    scratch = [pltpu.VMEM((rows, channels), BF16), pltpu.VMEM((rows, channels), F32), pltpu.VMEM((rows, channels), F32), pltpu.VMEM((half, width), BF16)]
    operands = (gained, flipped, scale, w_query, w_key, w_value, kvf, kvb, filters, w_out, flip)
    blocks = lax.axis_size("ctx")
    last_near = blocks // 2 - 1
    left = passed_along(kvf, 1, [i for i in range(1, blocks) if i != last_near])
    first, last, *early = call(early_kernel, [edge, edge] + inner_outs, scratch, 1_000_000, 300_000, operands)
    right = passed_along(first, -1, range(blocks - 1))
    late_left = passed_along(last, 1, [last_near])
    qf, pf, tf, wf, qb, pb, tb, wb = call(inner_kernel, inner_outs, scratch, 600_000_000, 300_000, operands + tuple(early))
    scratch = [pltpu.VMEM((half, channels), F32), pltpu.VMEM((half, channels), F32)]
    low = call(
        fore_kernel,
        [((half, 2 * channels), BF16), ((half, 2 * channels), BF16)],
        scratch,
        500_000_000,
        2_000_000,
        (left, qf, pf, tb, wf, filters),
    )
    keep, send = call(
        back_kernel,
        [((rows, 2 * channels), BF16), ((rows, 2 * channels), BF16)],
        scratch,
        500_000_000,
        2_000_000,
        (right, qb, pb, tf, wb, late_left, qf, pf, tb, wf, filters, *low),
    )
    place = lax.axis_index("tp")
    pair = lax.all_gather(send, "tp", axis_index_groups=CHIP_PAIRS)
    summed = keep.astype(F32) + jnp.where(place % 2 == 0, pair[1], pair[0]).astype(F32)
    both = lax.all_gather(summed[:, channels:].astype(BF16), "tp", axis_index_groups=CORE_PAIRS)
    received = jnp.where(place < 2, both[1], both[0]).astype(F32)
    return (hidden.astype(F32) + summed[:, :channels] + received).astype(BF16)


def solution(mesh):
    in_specs = (
        P("ctx", "tp"),
        P("ctx"),
        P(),
        P(),
        P(None, "tp"),
        P(None, "tp"),
        P(None, "tp"),
        P("tp", None),
        P(None, "tp"),
    )
    return jax.shard_map(on_device, mesh=mesh, in_specs=in_specs, out_specs=P("ctx", "tp"), check_vma=False)
```

```python
import jax
import jax.numpy as jnp
from jax import lax
from jax.experimental import pallas as pl
from jax.experimental.pallas import tpu as pltpu
from jax.sharding import PartitionSpec as P

K = 128
TILE = 8
STEPS = K // TILE
LANES = 128
GROUP = 4
F32 = jnp.float32
BF16 = jnp.bfloat16
CHIP_PAIRS = [[0, 1], [2, 3]]
CORE_PAIRS = [[0, 2], [1, 3]]


def passed_along(block, distance, receivers):
    return lax.ppermute(block, "ctx", [(i - distance, i) for i in receivers])


def anti_identity(size):
    rows = lax.broadcasted_iota(jnp.int32, (size, size), 0)
    columns = lax.broadcasted_iota(jnp.int32, (size, size), 1)
    return jnp.where(rows + columns == size - 1, 1.0, 0.0).astype(BF16)


def dot(left, right):
    return jnp.dot(left, right, preferred_element_type=F32)


def columns_reversed(block, flip, out_ref):
    width = flip.shape[0]
    parts = block.shape[1] // width
    for part in range(parts):
        source = block[:, (parts - 1 - part) * width : (parts - part) * width]
        out_ref[:, part * width : (part + 1) * width] = dot(source, flip).astype(BF16)


def project(source, scale, w_ref):
    return (dot(source, w_ref[...]) * scale).astype(BF16)


def keyval(source, scale, wk_ref, wv_ref):
    key = project(source, scale, wk_ref).astype(F32)
    value = project(source, scale, wv_ref).astype(F32)
    return (key * value).astype(BF16)


def prepare_kernel(bases_hbm, one_hot_ref, flip_ref, bases_ref, arrived):
    copy = pltpu.make_async_copy(bases_hbm, bases_ref, arrived)
    copy.start()
    flip_ref[...] = anti_identity(flip_ref.shape[0])
    copy.wait()
    base_rows = lax.broadcasted_iota(jnp.int32, one_hot_ref.shape, 0)
    one_hot_ref[...] = jnp.where(base_rows == bases_ref[...], 1.0, 0.0).astype(BF16)


def project_kernel(x_ref, one_hot_ref, table_ref, gain_ref, wk_ref, wv_ref, flip_ref, gained_ref, flipped_ref, scale_ref, kvf_ref, kvb_ref):
    half = kvf_ref.shape[0]
    embedded = lax.dot_general(one_hot_ref[...], table_ref[...], (((0,), (0,)), ((), ())), preferred_element_type=F32)
    summed = x_ref[...].astype(F32) + embedded
    gained = (summed * gain_ref[...]).astype(BF16)
    gained_ref[...] = gained
    scale = lax.rsqrt(jnp.mean(summed * summed, axis=1, keepdims=True) + 1e-06)
    scale_ref[...] = scale
    columns_reversed(gained[:half], flip_ref[...], flipped_ref)
    kvf_ref[...] = keyval(gained[half:], scale[half:], wk_ref, wv_ref)
    kvb_ref[...] = keyval(flipped_ref[...], scale[:half], wk_ref, wv_ref)


def tap_sums(source_ref, filters_ref, lanes, plan):
    acc = [[None] * len(plan) for _ in range(TILE)]
    for a in range(STEPS):
        starts = {i: dict(pairs)[a] for i, pairs in enumerate(plan) if a in dict(pairs)}
        blocks = {i: source_ref[pl.ds(start, TILE), lanes] for i, start in starts.items()}
        for b in range(TILE) if starts else ():
            tap = filters_ref[a * TILE + b : a * TILE + b + 1, lanes]
            for i, block in blocks.items():
                product = tap * block
                acc[b][i] = product if acc[b][i] is None else acc[b][i] + product
    return acc


def moved_sum(here, before, causal):
    row = lax.broadcasted_iota(jnp.int32, (TILE, LANES), 0)
    total = here[0]
    for b in range(1, TILE):
        if causal:
            picked = jnp.where(row < TILE - b, here[b], before[b])
            piece = pltpu.roll(picked, b, 0)
        else:
            picked = jnp.where(row >= b, here[b], before[b])
            piece = pltpu.roll(picked, TILE - b, 0)
        total = total + piece
    return total


def conv_local(source_ref, filters_ref, out_ref, causal):
    tiles = source_ref.shape[0] // TILE
    zero = jnp.zeros((TILE, LANES), F32)

    def row_of(u):
        return (u if causal else tiles - 1 - u) * TILE

    for lane_block in range(source_ref.shape[1] // LANES):
        lanes = slice(lane_block * LANES, (lane_block + 1) * LANES)

        def group(first, before, lanes, at):
            plan = [[(a, at(first + i - a)) for a in range(STEPS) if not isinstance(first, int) or first + i >= a] for i in range(GROUP)]
            acc = tap_sums(source_ref, filters_ref, lanes, plan)
            for i in range(GROUP):
                here = [acc[b][i] for b in range(TILE)]
                out_ref[pl.ds(at(first + i), TILE), lanes] = moved_sum(here, before, causal)
                before = here
            return before

        before = [zero] * TILE
        for g in range(STEPS // GROUP):
            before = group(g * GROUP, before, lanes, row_of)

        def step(g, carried, lanes=lanes, group=group):
            before = group(g * GROUP, [zero, *carried], lanes, lambda u: pl.multiple_of(row_of(u), TILE))
            return tuple(before[1:])

        lax.fori_loop(STEPS // GROUP, tiles // GROUP, step, tuple(before[1:]))


def conv_halo(source_ref, filters_ref, out_ref, causal):
    tiles = source_ref.shape[0] // TILE
    zero = jnp.zeros((TILE, LANES), F32)

    def row_of(u):
        return (u if causal else tiles - 1 - u) * TILE

    for lane_block in range(source_ref.shape[1] // LANES):
        lanes = slice(lane_block * LANES, (lane_block + 1) * LANES)
        before = [zero] * TILE
        for first in range(-1, tiles - 1, GROUP):
            plan = [[(a, row_of(tiles + u - a)) for a in range(u + 1, STEPS)] for u in range(first, first + GROUP)]
            acc = tap_sums(source_ref, filters_ref, lanes, plan)
            for i, u in enumerate(range(first, first + GROUP)):
                here = [acc[b][i] for b in range(TILE)]
                if u >= 0:
                    rows = slice(row_of(u), row_of(u) + TILE)
                    out_ref[rows, lanes] = out_ref[rows, lanes] + moved_sum(here, before, causal)
                before = here
        rows = slice(row_of(tiles - 1), row_of(tiles - 1) + TILE)
        out_ref[rows, lanes] = out_ref[rows, lanes] + moved_sum([zero] * TILE, before, causal)


def gate(query, conv_out):
    return (query.astype(F32) * conv_out).astype(BF16)


def blocks_after_far():
    return lax.axis_index("ctx") - lax.axis_size("ctx") // 2


def fore_early():
    after = blocks_after_far()
    return jnp.logical_and(after >= 0, after <= 1)


def back_early():
    return blocks_after_far() == 0


def ordered_chunks():
    place = lax.axis_index("tp")
    core = lax.rem(place, 2)
    chip = place // 2
    return [2 * at_chip + at_core for at_core in (core, 1 - core) for at_chip in (chip, 1 - chip)]


def inner_fore(operands, outs, query, source, conv):
    gained_ref, scale_ref, wq_ref, wk_ref, wv_ref, kvf_ref, filters_ref, wout_ref = operands
    q_ref, part_ref, term_ref, w_ref = outs
    half, width = kvf_ref.shape
    for part, number in enumerate(ordered_chunks()):
        w_ref[:, part * width : (part + 1) * width] = wout_ref[:, pl.ds(pl.multiple_of(number * width, width), width)]
    query[...] = project(gained_ref[...], scale_ref[...], wq_ref)
    q_ref[...] = query[:half]
    source[:half] = keyval(gained_ref[:half], scale_ref[:half], wk_ref, wv_ref).astype(F32)
    source[half:] = kvf_ref[...].astype(F32)
    conv_local(source, filters_ref, conv, True)
    part_ref[...] = conv[:half]
    term_ref[...] = dot(gate(query[half:], conv[half:]), w_ref[...])


def inner_back(operands, outs, query, source, conv, flipped):
    gained_ref, low_ref, scale_ref, wq_ref, wk_ref, wv_ref, kvb_ref, filters_ref, wout_ref, flip_ref = operands
    q_ref, part_ref, term_ref, w_ref = outs
    half, width = kvb_ref.shape
    for part, number in enumerate(ordered_chunks()):
        chunk = wout_ref[:, pl.ds(pl.multiple_of((3 - number) * width, width), width)]
        w_ref[:, part * width : (part + 1) * width] = dot(chunk, flip_ref[...]).astype(BF16)
    columns_reversed(gained_ref[half:], flip_ref[...], flipped)
    query[:half] = project(low_ref[...], scale_ref[:half], wq_ref)
    query[half:] = project(flipped[...], scale_ref[half:], wq_ref)
    q_ref[...] = query[half:]
    source[:half] = kvb_ref[...].astype(F32)
    source[half:] = keyval(flipped[...], scale_ref[half:], wk_ref, wv_ref).astype(F32)
    conv_local(source, filters_ref, conv, False)
    part_ref[...] = conv[half:]
    term_ref[...] = dot(gate(query[:half], conv[:half]), w_ref[...])


INPUTS = 11


def strands(inputs, outs, scratch):
    gained_ref, low_ref, scale_ref, wq_ref, wk_ref, wv_ref, kvf_ref, kvb_ref, filters_ref, wout_ref, flip_ref = inputs
    fore = (gained_ref, scale_ref, wq_ref, wk_ref, wv_ref, kvf_ref, filters_ref, wout_ref)
    back = (gained_ref, low_ref, scale_ref, wq_ref, wk_ref, wv_ref, kvb_ref, filters_ref, wout_ref, flip_ref)
    return lambda: inner_fore(fore, outs[:4], *scratch[:3]), lambda: inner_back(back, outs[4:], *scratch)


def early_kernel(*refs):
    inputs, first_ref, last_ref, rest = refs[:INPUTS], refs[INPUTS], refs[INPUTS + 1], refs[INPUTS + 2 :]
    fore, back = strands(inputs, rest[:8], rest[8:])
    first_ref[...] = inputs[7][...]
    last_ref[...] = inputs[6][...]
    pl.when(fore_early())(fore)
    pl.when(back_early())(back)


def inner_kernel(*refs):
    inputs, rest = refs[:INPUTS], refs[INPUTS:]
    early, outs, scratch = rest[:8], rest[8:16], rest[16:]
    fore, back = strands(inputs, outs, scratch)

    def copied(start):
        for i in range(start, start + 4):
            outs[i][...] = early[i][...]

    pl.when(fore_early())(lambda: copied(0))
    pl.when(back_early())(lambda: copied(4))
    pl.when(jnp.logical_not(fore_early()))(fore)
    pl.when(jnp.logical_not(back_early()))(back)


def outer(halo_ref, q_ref, part_ref, term_ref, w_ref, filters_ref, source, conv, causal):
    source[...] = halo_ref[...].astype(F32)
    conv[...] = part_ref[...]
    conv_halo(source, filters_ref, conv, causal)
    return term_ref[...] + dot(gate(q_ref[...], conv[...]), w_ref[...])


def fore(left_ref, qf_ref, pf_ref, tb_ref, wf_ref, filters_ref, keep_ref, send_ref, source, conv):
    half = left_ref.shape[0]
    width = keep_ref.shape[1]
    total = outer(left_ref, qf_ref, pf_ref, tb_ref, wf_ref, filters_ref, source, conv, True)
    keep_ref[:half] = total[:, :width]
    send_ref[:half] = total[:, width:].astype(BF16)


def before_far():
    return blocks_after_far() == -1


def fore_kernel(*refs):
    @pl.when(jnp.logical_not(before_far()))
    def _():
        fore(*refs)


def back_kernel(right_ref, qb_ref, pb_ref, tf_ref, wb_ref, late_ref, qf_ref, pf_ref, tb_ref, wf_ref, filters_ref, low_keep_ref, low_send_ref, keep_ref, send_ref, source, conv):
    half, width = low_keep_ref.shape

    @pl.when(before_far())
    def _():
        fore(late_ref, qf_ref, pf_ref, tb_ref, wf_ref, filters_ref, keep_ref, send_ref, source, conv)

    @pl.when(jnp.logical_not(before_far()))
    def _():
        keep_ref[:half] = low_keep_ref[...]
        send_ref[:half] = low_send_ref[...]

    total = outer(right_ref, qb_ref, pb_ref, tf_ref, wb_ref, filters_ref, source, conv, False)
    keep_ref[half:] = total[:, :width]
    send_ref[half:] = total[:, width:].astype(BF16)


def call(kernel, outs, scratch, flops, bytes_accessed, operands, in_hbm=()):
    vmem = pl.BlockSpec(memory_space=pltpu.VMEM)
    hbm = pl.BlockSpec(memory_space=pltpu.HBM)
    operands = [pltpu.with_memory_space_constraint(x, pltpu.HBM) if i in in_hbm else x for i, x in enumerate(operands)]
    return pl.pallas_call(
        kernel,
        out_shape=[jax.ShapeDtypeStruct(shape, kind) for shape, kind in outs],
        in_specs=[hbm if i in in_hbm else vmem for i in range(len(operands))],
        out_specs=[vmem] * len(outs),
        scratch_shapes=scratch,
        compiler_params=pltpu.CompilerParams(vmem_limit_bytes=32 * 1024 * 1024),
        cost_estimate=pl.CostEstimate(flops=flops, bytes_accessed=bytes_accessed, transcendentals=0),
    )(*operands)


def on_device(hidden, bases, base_table, norm_gain, w_query, w_key, w_value, w_out, filters):
    rows, channels = hidden.shape
    half = rows // 2
    width = w_query.shape[0]
    edge = ((half, channels), BF16)
    one_hot, flip = call(
        prepare_kernel,
        [((4, rows), BF16), ((channels, channels), BF16)],
        [pltpu.VMEM((1, rows), jnp.int32), pltpu.SemaphoreType.DMA(())],
        200_000_000,
        1_000,
        (bases.reshape(1, rows),),
        in_hbm=(0,),
    )
    shared, one_hot, flip = lax.optimization_barrier((hidden, one_hot, flip))
    gathered = lax.all_gather(shared, "tp", axis=1, tiled=True)
    gained, flipped, scale, kvf, kvb = call(
        project_kernel,
        [((rows, width), BF16), ((half, width), BF16), ((rows, 1), F32), edge, edge],
        [],
        600_000_000,
        4_000_000,
        (gathered, one_hot, base_table, norm_gain.reshape(1, width), w_key, w_value, flip),
    )
    partial = ((half, channels), F32)
    term = ((half, width), F32)
    weight = ((channels, width), BF16)
    inner_outs = [edge, partial, term, weight] * 2
    scratch = [pltpu.VMEM((rows, channels), BF16), pltpu.VMEM((rows, channels), F32), pltpu.VMEM((rows, channels), F32), pltpu.VMEM((half, width), BF16)]
    operands = (gained, flipped, scale, w_query, w_key, w_value, kvf, kvb, filters, w_out, flip)
    blocks = lax.axis_size("ctx")
    last_near = blocks // 2 - 1
    left = passed_along(kvf, 1, [i for i in range(1, blocks) if i != last_near])
    first, last, *early = call(early_kernel, [edge, edge] + inner_outs, scratch, 1_000_000, 300_000, operands)
    right = passed_along(first, -1, range(blocks - 1))
    late_left = passed_along(last, 1, [last_near])
    qf, pf, tf, wf, qb, pb, tb, wb = call(inner_kernel, inner_outs, scratch, 600_000_000, 300_000, operands + tuple(early))
    scratch = [pltpu.VMEM((half, channels), F32), pltpu.VMEM((half, channels), F32)]
    low = call(
        fore_kernel,
        [((half, 2 * channels), F32), ((half, 2 * channels), BF16)],
        scratch,
        500_000_000,
        2_000_000,
        (left, qf, pf, tb, wf, filters),
    )
    keep, send = call(
        back_kernel,
        [((rows, 2 * channels), F32), ((rows, 2 * channels), BF16)],
        scratch,
        500_000_000,
        2_000_000,
        (right, qb, pb, tf, wb, late_left, qf, pf, tb, wf, filters, *low),
    )
    place = lax.axis_index("tp")
    pair = lax.all_gather(send, "tp", axis_index_groups=CHIP_PAIRS)
    summed = keep + jnp.where(place % 2 == 0, pair[1], pair[0]).astype(F32)
    both = lax.all_gather(summed[:, channels:].astype(BF16), "tp", axis_index_groups=CORE_PAIRS)
    received = jnp.where(place < 2, both[1], both[0]).astype(F32)
    return (hidden.astype(F32) + summed[:, :channels] + received).astype(BF16)


def solution(mesh):
    in_specs = (
        P("ctx", "tp"),
        P("ctx"),
        P(),
        P(),
        P(None, "tp"),
        P(None, "tp"),
        P(None, "tp"),
        P("tp", None),
        P(None, "tp"),
    )
    return jax.shard_map(on_device, mesh=mesh, in_specs=in_specs, out_specs=P("ctx", "tp"), check_vma=False)
```
